512 devices in a mesh: patch: 64 (over y, z), band: 8 (over x, core).
Axes of the slice: x: 4, y: 8, z: 8, core: 2. Of those that a mesh axis runs over, the one named last changes fastest.
Arguments:
- visit_tiles: bfloat16 [8, 4096, 128, 128], P('band', 'patch'), may hold values from -8 to 8
- tile_patch: int32 [8, 4096, 1], P('band', 'patch'), may hold values from 0 to 63; in each aligned block of 64 rows (0 to 63, 64 to 127, ..., all dimensions but the last counted through in order) at most 2 rows name the same one
- tile_slot: int32 [8, 4096], P('band', 'patch'), may hold values from 0 to 3
- tile_weight: bfloat16 [8, 4096], P('band', 'patch'), may hold values from 0.5 to 4
- psf_coeff: bfloat16 [8, 4096, 27], P('band', 'patch'), may hold values from -4 to 4
Outputs:
- coadd_image: bfloat16 [8, 16384, 256], P('band', 'patch')
- detection: bfloat16 [8, 4096, 128, 128], P('band', 'patch')
- chi_image: bfloat16 [16384, 256], P('patch')
The draws below stay inside these ranges and needn't reach their ends.
Inputs may be any that keep to these rules, and one draw needn't show every extreme that they name: `tile_patch`: among the tiles of one device (aligned blocks of 64 tiles of a band), no patch is named more than 2 times, and in some block one patch is named exactly 2 times.
All inputs are finite; a program needn't handle non-finite values.
Results may differ from the reference program's by a relative error of at most 0.012.
Values may be sent and summed in bfloat16 or wider, within the bound.
No kernel may reach another device: no remote copies, remote signals or barrier semaphores. Data moves between devices by JAX's collectives and lax.ppermute only.
A program may use at most 64 MiB of HBM per device.

```python
import math
import jax
import jax.numpy as jnp
import numpy as np
from jax import lax

PIX = 128
KR = 10
NB = 27
SB = 2
TILES_DEV = 64
BANDS = 8
TILES = 4096
CAP = 2
SLOTS = 4
PR = 256
PC = 256
N_PATCH = 64


def draw_visit_tiles(key, part):
    key = jax.random.fold_in(key, 11)
    scene_key = jax.random.fold_in(key, 1)
    noise_key = jax.random.fold_in(key, 2)
    scene = 1.5 * jax.random.normal(scene_key, (PIX, PIX), jnp.float32)
    noise = 0.5 * jax.random.normal(noise_key, (BANDS, TILES, PIX, PIX), jnp.float32)
    values = jnp.clip(scene[None, None, :, :] + noise, -8.0, 8.0)
    return values.astype(jnp.bfloat16)


def touch_ends(values, stream_key, low, high):
    shape = values.shape
    index_at = [jax.random.randint(jax.random.fold_in(stream_key, axis), (), 0, shape[axis]) for axis in range(len(shape))]
    values = values.at[tuple(index_at)].set(low)
    longest = shape.index(max(shape))
    index_at[longest] = (index_at[longest] + 1) % shape[longest]
    return values.at[tuple(index_at)].set(high)


def block_scale(key, shape, split, smallest, largest):
    def one(dim, shards_of):
        steps = jax.random.uniform(jax.random.fold_in(jax.random.fold_in(key, 6), dim), (shards_of,), jnp.float32, smallest / len(split), largest / len(split))
        return jnp.repeat(jnp.exp(steps), shape[dim] // shards_of).reshape((-1,) + (1,) * (len(shape) - dim - 1))

    gain = one(*split[0])
    for cut in split[1:]:
        gain = gain * one(*cut)
    return gain


def deal_out(stream_key, own, number, rows, number_of, top, most, skew):
    sequence = jax.random.permutation(stream_key, number_of)
    packed, ordinary = shares(number_of, rows * top, most, skew, True), shares(number_of, rows * top, most, skew, False)
    places = jnp.arange(number_of)

    def named(tallies, rotation):
        used = int((tallies > 0).sum())
        fixed = max(1, used // 4)
        shifted = fixed + (places - fixed + rotation * (used - fixed)) % max(1, number_of - fixed)
        return jnp.zeros((number_of,), jnp.int32).at[sequence[jnp.where(places < fixed, places, shifted)]].set(jnp.asarray(tallies, jnp.int32))

    tallies = jnp.where(number % 4 == 0, named(packed, number // 4), named(ordinary, number - number // 4 - 1))
    mixed = jax.random.permutation(jax.random.fold_in(own, 3), number_of)
    source_of, receiver = mixed[0:number_of // 2 * 2:2], mixed[1:number_of // 2 * 2:2]
    room = jnp.minimum(tallies[source_of] - 1, most - tallies[receiver]) // 2
    room = jnp.where((source_of == sequence[0]) | (receiver == sequence[0]) | (tallies[receiver] == 0), 0, jnp.maximum(room, 0))
    shifted = jax.random.randint(jax.random.fold_in(own, 4), (number_of // 2,), 0, 1 << 20) % (room + 1)
    tallies = tallies.at[source_of].add(-shifted).at[receiver].add(shifted)
    items = jnp.searchsorted(jnp.cumsum(tallies), jnp.arange(rows * top), side="right").astype(jnp.int32)
    table = items.reshape(top, rows).T
    table = table[jax.random.permutation(jax.random.fold_in(own, 1), rows)]
    rotation = jax.random.randint(jax.random.fold_in(own, 2), (rows, 1), 0, top)
    return jnp.take_along_axis(table, (jnp.arange(top)[None, :] + rotation) % top, axis=1)


def shares(amount, total, reach, skew, full):
    loads = [(1 << 20) // math.isqrt(grade ** skew) + 1 for grade in range(1, amount + 1)]
    largest = reach if full else min(reach, max(-(-total // amount), total * loads[0] // sum(loads)))
    least = 1 if total - largest >= amount - 1 else 0
    given, spare = [largest] + [least] * (amount - 1), total - largest - least * (amount - 1)
    while spare > 0:
        free = [i for i in range(1, amount) if given[i] < largest] or [i for i in range(1, amount) if given[i] < reach]
        whole, budget = sum([loads[i] for i in free]), spare
        for i in free:
            extra = min(reach - given[i], max(1, budget * loads[i] // whole), spare)
            given[i] = given[i] + extra
            spare = spare - extra
    return np.array(given)


def scatter_about(own_key, extent, width, bound, pieces=(), dtype=jnp.bfloat16):
    drawn = jax.random.normal(own_key, extent, jnp.float32) * width
    if len(pieces) > 0:
        drawn = block_scale(own_key, extent, pieces, -0.22, 0.18) * drawn
    return jnp.clip(drawn, min=-bound, max=bound).astype(dtype)


def setup_inputs(seed: int = 0) -> dict:
    arg_keys = jax.random.split(jax.random.key(seed), 6)
    visit_tiles = draw_visit_tiles(jax.random.fold_in(arg_keys[5], 71), 0)
    tile_patch_keys = jax.random.split(jax.random.fold_in(arg_keys[1], 1), BANDS * TILES // TILES_DEV)
    tile_patch_turns = jax.random.permutation(jax.random.fold_in(arg_keys[1], 3), BANDS * TILES // TILES_DEV)
    tile_patch = jax.vmap(lambda own, number: deal_out(jax.random.fold_in(arg_keys[1], 2), own, number, TILES_DEV, N_PATCH, 1, CAP, 2))(tile_patch_keys, tile_patch_turns).reshape((BANDS, TILES, 1))
    tile_slot = touch_ends(jax.random.randint(arg_keys[2], (BANDS, TILES), 0, SLOTS), jax.random.fold_in(arg_keys[2], 1), 0, SLOTS - 1).astype(jnp.int32)
    tile_weight = jnp.clip(jnp.exp(math.log(4.0) - 2.0794415 * jax.random.uniform(arg_keys[3], (BANDS, TILES), jnp.float32) ** block_scale(arg_keys[3], (BANDS, TILES), ((0, 8), (1, 64)), -0.2, 0.2)), 0.5, 4.0).astype(jnp.bfloat16)
    psf_coeff = scatter_about(arg_keys[4], (BANDS, TILES, NB), 1.0, 4.0, ((0, 8), (1, 64)))
    return dict(visit_tiles=visit_tiles, tile_patch=tile_patch, tile_slot=tile_slot, tile_weight=tile_weight, psf_coeff=psf_coeff)


SIGMAS = (0.7, 1.5, 3.0)
DEGREES = (4, 2, 2)

def kernel_taps(sigma_value, exponent):
    offsets = jnp.arange(-KR, KR + 1).astype(jnp.float32)
    gaussian = jnp.exp(-offsets * offsets / (2.0 * sigma_value * sigma_value))
    return (gaussian * (offsets / sigma_value) ** exponent / jnp.sum(gaussian)).astype(jnp.bfloat16)

def smooth_taps():
    offsets = jnp.arange(-KR, KR + 1).astype(jnp.float32)
    gaussian = jnp.exp(-offsets * offsets / 8.0)
    return (gaussian / jnp.sum(gaussian)).astype(jnp.bfloat16)

def band_matrix(tap_table, row_total, col_total, offset_rows):
    distance = jnp.arange(col_total)[None, :] - jnp.arange(row_total)[:, None] - offset_rows
    matrix = jnp.zeros((row_total, col_total), jnp.float32)
    for offset in range(2 * KR + 1):
        matrix = jnp.where(distance == offset - KR, tap_table[offset].astype(jnp.float32), matrix)
    return matrix.astype(jnp.bfloat16)

def basis_list():
    listing = []
    for scale_index in range(len(SIGMAS)):
        for power_x in range(DEGREES[scale_index] + 1):
            for power_y in range(DEGREES[scale_index] + 1 - power_x):
                listing.append((scale_index, power_x, power_y))
    return listing

def shift_rows(field, tap_table):
    padded = jnp.pad(field, ((KR, KR), (0, 0)))
    running = jnp.zeros(field.shape, jnp.float32)
    for offset in range(2 * KR + 1):
        running = running + tap_table[offset].astype(jnp.float32) * padded[offset:offset + field.shape[0]]
    return running

def shift_cols(field, tap_table):
    padded = jnp.pad(field, ((0, 0), (KR, KR)))
    running = jnp.zeros(field.shape, jnp.float32)
    for offset in range(2 * KR + 1):
        running = running + tap_table[offset].astype(jnp.float32) * padded[:, offset:offset + field.shape[1]]
    return running

def to_blocks(field):
    return field.reshape(N_PATCH, SB, PIX, SB, PIX).transpose(0, 1, 3, 2, 4).reshape(N_PATCH * SLOTS, PIX * PIX)

def one_band(band_items):
    visit_tiles, tile_patch, tile_slot, tile_weight, psf_coeff = band_items
    slot_index = (tile_patch * SLOTS + tile_slot).astype(jnp.int32)
    weight_float = tile_weight.astype(jnp.float32)
    tile_rows = visit_tiles.reshape(TILES, PIX * PIX).astype(jnp.float32)
    numerator = jax.ops.segment_sum(weight_float[:, None] * tile_rows, slot_index, num_segments=N_PATCH * SLOTS)
    weight_sum = jax.ops.segment_sum(weight_float, slot_index, num_segments=N_PATCH * SLOTS)
    blocks = (numerator / jnp.maximum(weight_sum, 1.0)[:, None]).astype(jnp.bfloat16)
    band_image = blocks.reshape(N_PATCH, SB, SB, PIX, PIX).transpose(0, 1, 3, 2, 4).reshape(N_PATCH * PR, PC)
    coadd_float = band_image.astype(jnp.float32)
    vertical = {}
    for scale_index in range(len(SIGMAS)):
        for exponent in range(DEGREES[scale_index] + 1):
            tap_table = kernel_taps(SIGMAS[scale_index], exponent)
            vertical[scale_index, exponent] = shift_rows(coadd_float, tap_table).astype(jnp.bfloat16)
    matched = jnp.zeros((TILES, PIX * PIX), jnp.float32)
    for number, (scale_index, power_x, power_y) in enumerate(basis_list()):
        tap_table = kernel_taps(SIGMAS[scale_index], power_x)
        basis_image = shift_cols(vertical[scale_index, power_y].astype(jnp.float32), tap_table).astype(jnp.bfloat16)
        picked = to_blocks(basis_image)[slot_index]
        matched = matched + psf_coeff[:, number].astype(jnp.float32)[:, None] * picked.astype(jnp.float32)
    matched = matched.astype(jnp.bfloat16)
    difference = (tile_rows - matched.astype(jnp.float32)).astype(jnp.bfloat16).reshape(TILES, PIX, PIX)
    smoother = band_matrix(smooth_taps(), PIX, PIX, 0).astype(jnp.float32)
    across = jnp.einsum('rij,kj->rik', difference.astype(jnp.float32), smoother).astype(jnp.bfloat16)
    detection = jnp.einsum('ki,rij->rkj', smoother, across.astype(jnp.float32)).astype(jnp.bfloat16)
    weight_image = jnp.broadcast_to(weight_sum.reshape(N_PATCH, SB, 1, SB, 1), (N_PATCH, SB, PIX, SB, PIX)).reshape(N_PATCH * PR, PC)
    chi_terms = weight_image * coadd_float * coadd_float
    return (band_image, detection, chi_terms)

def reference(visit_tiles, tile_patch, tile_slot, tile_weight, psf_coeff):
    coadd_image, detection, chi_terms = lax.map(one_band, (visit_tiles, tile_patch[..., 0], tile_slot, tile_weight, psf_coeff))
    chi_image = jnp.sqrt(1.0 + lax.optimization_barrier(jnp.sum(chi_terms, axis=0))).astype(jnp.bfloat16)
    return (coadd_image, detection, chi_image)
```

```python
import functools

import jax
import jax.numpy as jnp
import ml_dtypes
import numpy as np
from jax import lax
from jax.experimental import pallas as pl
from jax.experimental.pallas import tpu as pltpu
from jax.sharding import PartitionSpec as P

KR = 10
SB = 2
PIX = 128
HALF = 64
HALO = 16
SPAN = HALF + HALO
BINS = 256
GROUP = 4
NB = 27
SIGMAS = (0.7, 1.5, 3.0)
DEGREES = (4, 2, 2)
BF16 = jnp.bfloat16
F32 = jnp.float32

PAIRS = [(s, p) for s in range(3) for p in range(DEGREES[s] + 1)]
BASIS = [
    (s, i, j)
    for s in range(3)
    for i in range(DEGREES[s] + 1)
    for j in range(DEGREES[s] + 1 - i)
]


def rounded(values):
    return np.asarray(values, np.float32).astype(ml_dtypes.bfloat16)


def kernel_taps(sigma_value, exponent):
    offsets = np.arange(-KR, KR + 1).astype(np.float32)
    gaussian = np.exp(-offsets * offsets / np.float32(2.0 * sigma_value * sigma_value))
    taps = gaussian * (offsets / np.float32(sigma_value)) ** exponent / np.sum(gaussian)
    return rounded(taps).astype(np.float64)


def smooth_taps():
    offsets = np.arange(-KR, KR + 1).astype(np.float32)
    gaussian = np.exp(-offsets * offsets / np.float32(8.0))
    return rounded(gaussian / np.sum(gaussian)).astype(np.float64)


def tap_matrix(taps, source, target):
    distance = source[:, None] - target[None, :]
    inside = np.abs(distance) <= KR
    return np.where(inside, taps[np.clip(distance + KR, 0, 2 * KR)], 0.0)


def constants():
    pixel = np.arange(PIX)
    smoother = tap_matrix(smooth_taps(), pixel, pixel)
    columns = np.concatenate([pixel, PIX + np.arange(64), np.arange(64) - 64])
    across = np.concatenate(
        [tap_matrix(kernel_taps(SIGMAS[s], i), columns, pixel) @ smoother.T for s, i in PAIRS], axis=1
    )
    upper_rows = np.concatenate([np.arange(HALF), PIX + np.arange(HALO)])
    lower_rows = np.concatenate([np.arange(HALO) - HALO, HALF + np.arange(HALF)])
    down = [
        np.concatenate(
            [-(smoother @ tap_matrix(kernel_taps(SIGMAS[s], j), rows, pixel).T) for s, j in PAIRS],
            axis=1,
        )
        for rows in (upper_rows, lower_rows)
    ]
    upper = np.concatenate([down[0], smoother], axis=1)
    return rounded(across), rounded(upper), rounded(down[1]), rounded(smoother.T)


def exchange_matrix():
    order = np.arange(256).reshape(16, 16).T.reshape(256)
    return np.eye(256, dtype=np.float32)[order].astype(ml_dtypes.bfloat16)


def swap_blocks(exchange, read, write, count):
    for first in range(0, count, 2):
        pair = jnp.concatenate(
            [read(first).reshape(256, PIX), read(first + 1).reshape(256, PIX)], axis=1
        )
        moved = jnp.dot(exchange, pair, preferred_element_type=F32).astype(BF16)
        write(first, moved[:, :PIX].reshape(16, 16, PIX))
        write(first + 1, moved[:, PIX:].reshape(16, 16, PIX))


def pack_kernel(exchange_ref, tile_ref, out_ref):
    exchange = exchange_ref[...]

    def read(block):
        return tile_ref[:, block * 16 : block * 16 + 16, :]

    def write(block, value):
        out_ref[block * 16 : block * 16 + 16, :, :] = value

    swap_blocks(exchange, read, write, HALF // 16)


def pack(exchange, tiles, half):
    count = tiles.shape[0]
    return pl.pallas_call(
        pack_kernel,
        grid=(count // 16,),
        in_specs=[
            pl.BlockSpec((256, 256), lambda g: (0, 0)),
            pl.BlockSpec((16, HALF, PIX), lambda g: (g, half, 0)),
        ],
        out_specs=pl.BlockSpec((HALF, 16, PIX), lambda g: (0, g, 0)),
        out_shape=jax.ShapeDtypeStruct((HALF, count, PIX), BF16),
        cost_estimate=pl.CostEstimate(
            flops=2 * 256 * count * HALF * PIX, bytes_accessed=4 * count * HALF * PIX, transcendentals=0
        ),
    )(exchange, tiles)


CHUNK = 512


def coadd_kernel(bin_ref, weight_ref, row_ref, coadd_ref, sum_ref):
    total = row_ref.shape[0]
    numbers = lax.broadcasted_iota(jnp.int32, (BINS, CHUNK), 0)
    ones = jnp.ones((CHUNK, PIX), BF16)
    running = jnp.zeros((BINS, 2 * PIX), F32)
    for start in range(0, total, CHUNK):
        match = bin_ref[:, start : start + CHUNK] == numbers
        loading = jnp.where(match, weight_ref[:, start : start + CHUNK], 0.0).astype(BF16)
        values = jnp.concatenate([row_ref[start : start + CHUNK, :], ones], axis=1)
        running = running + jnp.dot(loading, values, preferred_element_type=F32)
    weight_sum = running[:, PIX:]
    coadd_ref[...] = (running[:, :PIX] / jnp.maximum(weight_sum, 1.0)).astype(BF16)
    sum_ref[...] = weight_sum


def coadd_rows(bins, weights, rows):
    total = rows.shape[0]
    return pl.pallas_call(
        coadd_kernel,
        out_shape=(
            jax.ShapeDtypeStruct((BINS, PIX), BF16),
            jax.ShapeDtypeStruct((BINS, PIX), F32),
        ),
        compiler_params=pltpu.CompilerParams(vmem_limit_bytes=24 * 1024 * 1024),
        cost_estimate=pl.CostEstimate(
            flops=4 * BINS * total * PIX, bytes_accessed=2 * total * PIX, transcendentals=0
        ),
    )(bins, weights, rows)


def detect_kernel(
    upper,
    place_ref,
    coeff_ref,
    exchange_ref,
    gathered_ref,
    other_ref,
    across_ref,
    down_ref,
    smoother_ref,
    out_ref,
    image_ref,
    window_ref,
    mixed_ref,
):
    exchange = exchange_ref[...]
    lane = lax.broadcasted_iota(jnp.int32, (SPAN, PIX), 1)
    row = lax.broadcasted_iota(jnp.int32, (SPAN, PIX), 0)
    tile_count = out_ref.shape[0]

    def regroup(block, carry):
        base = pl.multiple_of(block * 16, 16)

        def read(number):
            return gathered_ref[number * 16 : number * 16 + 16, pl.ds(base, 16), :]

        def write(number, value):
            image_ref[pl.ds(base, 16), number * 16 : number * 16 + 16, :] = value

        swap_blocks(exchange, read, write, HALF // 16)
        return carry

    lax.fori_loop(0, BINS // 16, regroup, 0)

    def group(number, carry):
        for local in range(GROUP):
            place = place_ref[number * GROUP + local]
            column = place // 128
            level = place % 128
            own = image_ref[place]
            beside_place = place + 128 - 256 * column
            beside = image_ref[beside_place]
            if upper:
                step, edge = 1, level == 127
                own_edge = image_ref[jnp.where(edge, place, place + step), 0:HALO, :]
                beside_edge = image_ref[jnp.where(edge, beside_place, beside_place + step), 0:HALO, :]
                own = jnp.concatenate([own, own_edge], axis=0)
                beside = jnp.concatenate([beside, beside_edge], axis=0)
                outside = edge & (row >= HALF)
            else:
                step, edge = -1, level == 0
                own_edge = image_ref[jnp.where(edge, place, place + step), HALF - HALO : HALF, :]
                beside_edge = image_ref[
                    jnp.where(edge, beside_place, beside_place + step), HALF - HALO : HALF, :
                ]
                own = jnp.concatenate([own_edge, own], axis=0)
                beside = jnp.concatenate([beside_edge, beside], axis=0)
                outside = edge & (row < HALO)
            wrong_side = (lane // 64) != column
            zero = jnp.zeros((SPAN, PIX), F32)
            own = jnp.where(outside, zero, own.astype(F32))
            beside = jnp.where(outside | wrong_side, zero, beside.astype(F32))
            window_ref[local * SPAN : (local + 1) * SPAN, 0:PIX] = own.astype(BF16)
            window_ref[local * SPAN : (local + 1) * SPAN, PIX:] = beside.astype(BF16)
        window = window_ref[...]
        for scale in range(3):
            members = [k for k, pair in enumerate(PAIRS) if pair[0] == scale]
            first, last = members[0], members[-1] + 1
            filtered = jnp.dot(
                window, across_ref[:, first * PIX : last * PIX], preferred_element_type=F32
            )
            for local in range(GROUP):
                rows = slice(local * SPAN, (local + 1) * SPAN)
                base = (number * GROUP + local) * NB
                for power_y in range(DEGREES[scale] + 1):
                    total = None
                    for power_x in range(DEGREES[scale] + 1 - power_y):
                        scalar = coeff_ref[base + BASIS.index((scale, power_x, power_y))]
                        term = scalar * filtered[rows, power_x * PIX : (power_x + 1) * PIX]
                        total = term if total is None else total + term
                    spot = (first + power_y) * SPAN
                    mixed_ref[spot : spot + SPAN, local * PIX : (local + 1) * PIX] = total.astype(BF16)
        begin = pl.multiple_of(number * GROUP, GROUP)
        if upper:
            tiles = other_ref[pl.ds(begin, GROUP)].reshape(GROUP * PIX, PIX)
            smooth = jnp.dot(tiles, smoother_ref[...], preferred_element_type=F32).astype(BF16)
            spot = len(PAIRS) * SPAN
            for local in range(GROUP):
                mixed_ref[spot : spot + PIX, local * PIX : (local + 1) * PIX] = smooth[
                    local * PIX : (local + 1) * PIX
                ]
        result = jnp.dot(down_ref[...], mixed_ref[...], preferred_element_type=F32)
        for local in range(GROUP):
            piece = result[:, local * PIX : (local + 1) * PIX]
            if not upper:
                piece = piece + other_ref[begin + local]
            out_ref[begin + local] = piece.astype(out_ref.dtype)
        return carry

    lax.fori_loop(0, tile_count // GROUP, group, 0)


def detect_half(upper, place, coeff, exchange, gathered, other, across, down, smoother):
    tile_count = other.shape[0]
    depth = down.shape[1]
    smem = pl.BlockSpec(memory_space=pltpu.SMEM)
    vmem = pl.BlockSpec(memory_space=pltpu.VMEM)
    return pl.pallas_call(
        functools.partial(detect_kernel, upper),
        in_specs=[smem, smem] + [vmem] * 6,
        out_specs=vmem,
        out_shape=jax.ShapeDtypeStruct((tile_count, PIX, PIX), F32 if upper else BF16),
        scratch_shapes=[
            pltpu.VMEM((BINS, HALF, PIX), BF16),
            pltpu.VMEM((GROUP * SPAN, 2 * PIX), BF16),
            pltpu.VMEM((depth, GROUP * PIX), BF16),
        ],
        compiler_params=pltpu.CompilerParams(vmem_limit_bytes=40 * 1024 * 1024),
        cost_estimate=pl.CostEstimate(
            flops=2 * tile_count * (SPAN * 256 * 1408 + depth * PIX * PIX),
            bytes_accessed=12 * 1024 * 1024,
            transcendentals=0,
        ),
    )(place, coeff, exchange, gathered, other, across, down, smoother)


def body(visit_tiles, tile_patch, tile_slot, tile_weight, psf_coeff):
    tile_count = visit_tiles.shape[1]
    tiles = visit_tiles[0]
    across, upper, lower, smoother = (jnp.asarray(m) for m in constants())
    exchange = jnp.asarray(exchange_matrix())
    place = (tile_slot[0] % 2) * 128 + 2 * tile_patch[0, :, 0] + tile_slot[0] // 2
    about = jnp.concatenate([place.astype(F32), tile_weight[0].astype(F32)]).reshape(1, 2 * tile_count)
    about = lax.all_gather(about, "patch", axis=0, tiled=True)
    bins = about[:, :tile_count].astype(jnp.int32).reshape(1, -1)
    weights = about[:, tile_count:].reshape(1, -1)
    coeff = psf_coeff[0].astype(F32).reshape(-1)

    def rows_of(packed):
        return lax.all_to_all(packed, "patch", split_axis=0, concat_axis=0, tiled=True).reshape(-1, PIX)

    first_rows = rows_of(pack(exchange, tiles, 0))
    first_coadd, weight_sum = coadd_rows(bins, weights, first_rows)
    second_packed, first_coadd = lax.optimization_barrier((pack(exchange, tiles, 1), first_coadd))
    first_gathered = lax.all_gather(first_coadd, "patch", axis=0, tiled=False)
    second_rows = rows_of(second_packed)
    second_coadd, _ = coadd_rows(bins, weights, second_rows)
    second_gathered = lax.all_gather(second_coadd, "patch", axis=0, tiled=False)

    partial = detect_half(
        True, place, coeff, exchange, first_gathered, tiles, across, upper, smoother
    )
    detection = detect_half(
        False, place, coeff, exchange, second_gathered, partial, across, lower, smoother
    )

    patch = lax.axis_index("patch")

    def own_part(gathered):
        shaped = gathered.reshape(HALF, 2, 128, PIX)
        return lax.dynamic_slice_in_dim(shaped, 2 * patch, 2, axis=2).transpose(2, 0, 1, 3)

    coadd_image = jnp.stack([own_part(first_gathered), own_part(second_gathered)], axis=1)
    own_sum = lax.dynamic_slice_in_dim(weight_sum.reshape(2, 128, PIX), 2 * patch, 2, axis=1)
    own_sum = own_sum.transpose(1, 0, 2)[:, None, None]
    coadd_float = coadd_image.astype(F32)
    terms = (own_sum * coadd_float * coadd_float).reshape(SB * PIX, SB * PIX).astype(BF16)
    terms = lax.all_gather(terms, "band", axis=0, tiled=False)
    chi_image = jnp.sqrt(1.0 + jnp.sum(terms.astype(F32), axis=0)).astype(BF16)
    return (coadd_image.reshape(1, SB * PIX, SB * PIX), detection[None], chi_image)


def solution(mesh):
    return jax.shard_map(
        body,
        mesh=mesh,
        in_specs=(
            P("band", "patch", None, None),
            P("band", "patch", None),
            P("band", "patch"),
            P("band", "patch"),
            P("band", "patch", None),
        ),
        out_specs=(P("band", "patch", None), P("band", "patch", None, None), P("patch", None)),
        check_vma=False,
    )
```

```python
import jax
import jax.numpy as jnp
import ml_dtypes
import numpy as np
from jax import lax
from jax.experimental import pallas as pl
from jax.experimental.pallas import tpu as pltpu
from jax.sharding import PartitionSpec as P

KR = 10
SB = 2
PIX = 128
HALF = 64
HALO = 16
SPAN = PIX + 2 * HALO
META = 16
BINS = 256
GROUP = 4
NB = 27
SIGMAS = (0.7, 1.5, 3.0)
DEGREES = (4, 2, 2)
BF16 = jnp.bfloat16
F32 = jnp.float32

PAIRS = [(s, p) for s in range(3) for p in range(DEGREES[s] + 1)]
BASIS = [
    (s, i, j)
    for s in range(3)
    for i in range(DEGREES[s] + 1)
    for j in range(DEGREES[s] + 1 - i)
]


def rounded(values):
    return np.asarray(values, np.float32).astype(ml_dtypes.bfloat16)


def kernel_taps(sigma_value, exponent):
    offsets = np.arange(-KR, KR + 1).astype(np.float32)
    gaussian = np.exp(-offsets * offsets / np.float32(2.0 * sigma_value * sigma_value))
    taps = gaussian * (offsets / np.float32(sigma_value)) ** exponent / np.sum(gaussian)
    return rounded(taps).astype(np.float64)


def smooth_taps():
    offsets = np.arange(-KR, KR + 1).astype(np.float32)
    gaussian = np.exp(-offsets * offsets / np.float32(8.0))
    return rounded(gaussian / np.sum(gaussian)).astype(np.float64)


def tap_matrix(taps, source, target):
    distance = source[:, None] - target[None, :]
    inside = np.abs(distance) <= KR
    return np.where(inside, taps[np.clip(distance + KR, 0, 2 * KR)], 0.0)


def constants():
    pixel = np.arange(PIX)
    smoother = tap_matrix(smooth_taps(), pixel, pixel)
    columns = np.concatenate([pixel, PIX + np.arange(64), np.arange(64) - 64])
    across = np.concatenate(
        [tap_matrix(kernel_taps(SIGMAS[s], i), columns, pixel) @ smoother.T for s, i in PAIRS], axis=1
    )
    rows = np.arange(SPAN) - HALO
    down = [-(smoother @ tap_matrix(kernel_taps(SIGMAS[s], j), rows, pixel).T) for s, j in PAIRS]
    return rounded(across), rounded(np.concatenate(down + [smoother], axis=1)), rounded(smoother.T)


def exchange_matrix():
    order = np.arange(256).reshape(16, 16).T.reshape(256)
    return np.eye(256, dtype=np.float32)[order].astype(ml_dtypes.bfloat16)


def swap_blocks(exchange, read, write, count):
    for first in range(0, count, 2):
        pair = jnp.concatenate(
            [read(first).reshape(256, PIX), read(first + 1).reshape(256, PIX)], axis=1
        )
        moved = jnp.dot(exchange, pair, preferred_element_type=F32).astype(BF16)
        write(first, moved[:, :PIX].reshape(16, 16, PIX))
        write(first + 1, moved[:, PIX:].reshape(16, 16, PIX))


def pack_kernel(exchange_ref, about_ref, tile_ref, out_ref):
    step = pl.program_id(0)

    @pl.when(step < pl.num_programs(0) - 1)
    def _():
        def read(block):
            return tile_ref[:, block * 16 : block * 16 + 16, :]

        def write(block, value):
            out_ref[block * 16 : block * 16 + 16, :, :] = value

        swap_blocks(exchange_ref[...], read, write, HALF // 16)

    @pl.when(step == pl.num_programs(0) - 1)
    def _():
        out_ref[...] = jnp.broadcast_to(about_ref[...][None], out_ref.shape)


def pack(exchange, about, tiles):
    count = tiles.shape[0]
    parts = count // 16
    return pl.pallas_call(
        pack_kernel,
        grid=(2 * parts + 1,),
        in_specs=[
            pl.BlockSpec((256, 256), lambda g: (0, 0)),
            pl.BlockSpec((META, PIX), lambda g: (0, 0)),
            pl.BlockSpec(
                (16, HALF, PIX), lambda g: (g % parts, jnp.minimum(g // parts, 1), 0)
            ),
        ],
        out_specs=pl.BlockSpec((HALF, 16, PIX), lambda g: (0, g, 0)),
        out_shape=jax.ShapeDtypeStruct((HALF, 2 * count + META, PIX), BF16),
        cost_estimate=pl.CostEstimate(
            flops=4 * 256 * count * HALF * PIX, bytes_accessed=8 * count * HALF * PIX, transcendentals=0
        ),
    )(exchange, about, tiles)


def coadd_kernel(row_ref, coadd_ref, sum_ref):
    sources = row_ref.shape[0]
    count = (row_ref.shape[1] - META) // 2
    numbers = lax.broadcasted_iota(jnp.int32, (BINS, PIX), 0).astype(F32)
    ones = jnp.ones((4 * count, PIX), BF16)
    running = jnp.zeros((BINS, 3 * PIX), F32)
    for first in range(0, sources, 4):
        loading = []
        for source in (first, first + 2):
            about = row_ref[source, 2 * count :, :].astype(F32) + row_ref[source + 1, 2 * count :, :].astype(F32)
            loading.append(jnp.where(about[0:1] == numbers, about[1:2], 0.0).astype(BF16))
        values = jnp.concatenate(
            [
                row_ref[first : first + 4, 0:count, :].reshape(4 * count, PIX),
                row_ref[first : first + 4, count : 2 * count, :].reshape(4 * count, PIX),
                ones,
            ],
            axis=1,
        )
        running = running + jnp.dot(
            jnp.concatenate(loading, axis=1), values, preferred_element_type=F32
        )
    weight_sum = running[:, 2 * PIX :]
    scale = jnp.maximum(weight_sum, 1.0)
    coadd_ref[0:BINS, :] = (running[:, :PIX] / scale).astype(BF16)
    coadd_ref[BINS:, :] = (running[:, PIX : 2 * PIX] / scale).astype(BF16)
    sum_ref[...] = weight_sum


def coadd_rows(rows):
    return pl.pallas_call(
        coadd_kernel,
        out_shape=(
            jax.ShapeDtypeStruct((2 * BINS, PIX), BF16),
            jax.ShapeDtypeStruct((BINS, PIX), F32),
        ),
        compiler_params=pltpu.CompilerParams(vmem_limit_bytes=24 * 1024 * 1024),
        cost_estimate=pl.CostEstimate(
            flops=6 * BINS * 4096 * PIX, bytes_accessed=4 * 4096 * PIX, transcendentals=0
        ),
    )(rows)


def detect_kernel(
    place_ref,
    coeff_ref,
    exchange_ref,
    gathered_ref,
    tile_ref,
    across_ref,
    down_ref,
    smoother_ref,
    out_ref,
    image_ref,
    window_ref,
    mixed_ref,
):
    exchange = exchange_ref[...]
    lane = lax.broadcasted_iota(jnp.int32, (SPAN, PIX), 1)
    row = lax.broadcasted_iota(jnp.int32, (SPAN, PIX), 0)
    tile_count = out_ref.shape[0]

    def regroup(block, carry):
        base = pl.multiple_of(block * 16, 16)
        for half in range(2):

            def read(number):
                start = pl.multiple_of(base + half * BINS, 16)
                return gathered_ref[number * 16 : number * 16 + 16, pl.ds(start, 16), :]

            def write(number, value):
                spot = half * HALF + number * 16
                image_ref[pl.ds(base, 16), spot : spot + 16, :] = value

            swap_blocks(exchange, read, write, HALF // 16)
        return carry

    lax.fori_loop(0, BINS // 16, regroup, 0)

    def group(number, carry):
        for local in range(GROUP):
            place = place_ref[number * GROUP + local]
            column = place // 128
            level = place % 128
            other = place + 128 - 256 * column
            outside = ((level == 0) & (row < HALO)) | ((level == 127) & (row >= HALO + PIX))
            wrong_side = (lane // 64) != column
            back = jnp.where(level == 0, 0, 1)
            ahead = jnp.where(level == 127, 0, 1)
            for spot, block, unwanted in ((0, place, outside), (PIX, other, outside | wrong_side)):
                value = jnp.concatenate(
                    [
                        image_ref[block - back, PIX - HALO :, :],
                        image_ref[block],
                        image_ref[block + ahead, 0:HALO, :],
                    ],
                    axis=0,
                )
                value = jnp.where(unwanted, 0.0, value.astype(F32)).astype(BF16)
                window_ref[local * SPAN : (local + 1) * SPAN, spot : spot + PIX] = value
        window = window_ref[...]
        for scale in range(3):
            members = [k for k, pair in enumerate(PAIRS) if pair[0] == scale]
            first, last = members[0], members[-1] + 1
            filtered = jnp.dot(
                window, across_ref[:, first * PIX : last * PIX], preferred_element_type=F32
            )
            for local in range(GROUP):
                rows = slice(local * SPAN, (local + 1) * SPAN)
                base = (number * GROUP + local) * NB
                for power_y in range(DEGREES[scale] + 1):
                    total = None
                    for power_x in range(DEGREES[scale] + 1 - power_y):
                        scalar = coeff_ref[base + BASIS.index((scale, power_x, power_y))]
                        term = scalar * filtered[rows, power_x * PIX : (power_x + 1) * PIX]
                        total = term if total is None else total + term
                    spot = (first + power_y) * SPAN
                    mixed_ref[spot : spot + SPAN, local * PIX : (local + 1) * PIX] = total.astype(BF16)
        begin = pl.multiple_of(number * GROUP, GROUP)
        tiles = tile_ref[pl.ds(begin, GROUP)].reshape(GROUP * PIX, PIX)
        smooth = jnp.dot(tiles, smoother_ref[...], preferred_element_type=F32).astype(BF16)
        spot = len(PAIRS) * SPAN
        for local in range(GROUP):
            mixed_ref[spot : spot + PIX, local * PIX : (local + 1) * PIX] = smooth[
                local * PIX : (local + 1) * PIX
            ]
        result = jnp.dot(down_ref[...], mixed_ref[...], preferred_element_type=F32)
        for local in range(GROUP):
            out_ref[begin + local] = result[:, local * PIX : (local + 1) * PIX].astype(BF16)
        return carry

    lax.fori_loop(0, tile_count // GROUP, group, 0)


def detect(place, coeff, exchange, gathered, tiles, across, down, smoother):
    tile_count = tiles.shape[0]
    depth = down.shape[1]
    smem = pl.BlockSpec(memory_space=pltpu.SMEM)
    vmem = pl.BlockSpec(memory_space=pltpu.VMEM)
    return pl.pallas_call(
        detect_kernel,
        in_specs=[smem, smem] + [vmem] * 6,
        out_specs=vmem,
        out_shape=jax.ShapeDtypeStruct((tile_count, PIX, PIX), BF16),
        scratch_shapes=[
            pltpu.VMEM((BINS, PIX, PIX), BF16),
            pltpu.VMEM((GROUP * SPAN, 2 * PIX), BF16),
            pltpu.VMEM((depth, GROUP * PIX), BF16),
        ],
        compiler_params=pltpu.CompilerParams(vmem_limit_bytes=48 * 1024 * 1024),
        cost_estimate=pl.CostEstimate(
            flops=2 * tile_count * (SPAN * 256 * 1408 + depth * PIX * PIX),
            bytes_accessed=12 * 1024 * 1024,
            transcendentals=0,
        ),
    )(place, coeff, exchange, gathered, tiles, across, down, smoother)


def body(visit_tiles, tile_patch, tile_slot, tile_weight, psf_coeff):
    tiles = visit_tiles[0]
    across, down, smoother = (jnp.asarray(m) for m in constants())
    exchange = jnp.asarray(exchange_matrix())
    patch = lax.axis_index("patch")
    patch_count = lax.axis_size("patch")
    band_count = lax.axis_size("band")
    place = (tile_slot[0] % 2) * 128 + 2 * tile_patch[0, :, 0] + tile_slot[0] // 2
    facts = jnp.stack([place.astype(F32), tile_weight[0].astype(F32)])
    even = (patch % 2) == 0
    facts = jnp.concatenate([jnp.where(even, facts, 0.0), jnp.where(even, 0.0, facts)], axis=1)
    about = jnp.pad(facts, ((0, META - 2), (0, 0))).astype(BF16)
    coeff = psf_coeff[0].astype(F32).reshape(-1)

    def exchanged(array, axis):
        return lax.all_to_all(array, axis, split_axis=0, concat_axis=0, tiled=True)

    rows = exchanged(pack(exchange, about, tiles), "patch")
    coadd, weight_sum = coadd_rows(rows)
    gathered = lax.all_gather(coadd, "patch", axis=0, tiled=False)

    own = coadd.reshape(4, patch_count, 2, PIX).transpose(1, 0, 2, 3).reshape(patch_count, 8, PIX)
    own = exchanged(own, "patch").reshape(HALF, 2, 2, 2, PIX)
    coadd_image = own.transpose(3, 1, 0, 2, 4)
    own_sum = lax.dynamic_slice_in_dim(weight_sum.reshape(2, 128, PIX), 2 * patch, 2, axis=1)
    own_sum = own_sum.transpose(1, 0, 2)[:, None, None]
    coadd_float = coadd_image.astype(F32)
    terms = (own_sum * coadd_float * coadd_float).reshape(SB * PIX, SB * PIX).astype(BF16)
    terms = exchanged(jnp.broadcast_to(terms[None], (band_count,) + terms.shape), "band")
    chi_image = jnp.sqrt(1.0 + jnp.sum(terms.astype(F32), axis=0)).astype(BF16)
    coadd_image = coadd_image.reshape(1, SB * PIX, SB * PIX)

    gathered, chi_image, coadd_image = lax.optimization_barrier((gathered, chi_image, coadd_image))
    detection = detect(place, coeff, exchange, gathered, tiles, across, down, smoother)
    return (coadd_image, detection[None], chi_image)


def solution(mesh):
    return jax.shard_map(
        body,
        mesh=mesh,
        in_specs=(
            P("band", "patch", None, None),
            P("band", "patch", None),
            P("band", "patch"),
            P("band", "patch"),
            P("band", "patch", None),
        ),
        out_specs=(P("band", "patch", None), P("band", "patch", None, None), P("patch", None)),
        check_vma=False,
    )
```

```python
import functools

import jax
import jax.numpy as jnp
import ml_dtypes
import numpy as np
from jax import lax
from jax.experimental import pallas as pl
from jax.experimental.pallas import tpu as pltpu
from jax.sharding import PartitionSpec as P

KR = 10
SB = 2
PIX = 128
HALF = 64
HALO = 16
SPAN = PIX + 2 * HALO
META = 16
BINS = 256
GROUP = 4
BUFFERS = 2
NB = 27
SIGMAS = (0.7, 1.5, 3.0)
DEGREES = (4, 2, 2)
BF16 = jnp.bfloat16
F32 = jnp.float32

PAIRS = [(s, p) for s in range(3) for p in range(DEGREES[s] + 1)]
BASIS = [
    (s, i, j)
    for s in range(3)
    for i in range(DEGREES[s] + 1)
    for j in range(DEGREES[s] + 1 - i)
]


def rounded(values):
    return np.asarray(values, np.float32).astype(ml_dtypes.bfloat16)


def kernel_taps(sigma_value, exponent):
    offsets = np.arange(-KR, KR + 1).astype(np.float32)
    gaussian = np.exp(-offsets * offsets / np.float32(2.0 * sigma_value * sigma_value))
    taps = gaussian * (offsets / np.float32(sigma_value)) ** exponent / np.sum(gaussian)
    return rounded(taps).astype(np.float64)


def smooth_taps():
    offsets = np.arange(-KR, KR + 1).astype(np.float32)
    gaussian = np.exp(-offsets * offsets / np.float32(8.0))
    return rounded(gaussian / np.sum(gaussian)).astype(np.float64)


def tap_matrix(taps, source, target):
    distance = source[:, None] - target[None, :]
    inside = np.abs(distance) <= KR
    return np.where(inside, taps[np.clip(distance + KR, 0, 2 * KR)], 0.0)


def constants():
    pixel = np.arange(PIX)
    smoother = tap_matrix(smooth_taps(), pixel, pixel)
    columns = np.concatenate([pixel, PIX + np.arange(64), np.arange(64) - 64])
    across = np.concatenate(
        [tap_matrix(kernel_taps(SIGMAS[s], i), columns, pixel) @ smoother.T for s, i in PAIRS], axis=1
    )
    rows = np.arange(SPAN) - HALO
    down = [-(smoother @ tap_matrix(kernel_taps(SIGMAS[s], j), rows, pixel).T) for s, j in PAIRS]
    return rounded(across), rounded(np.concatenate(down + [smoother], axis=1)), rounded(smoother.T)


def exchange_matrix():
    order = np.arange(256).reshape(16, 16).T.reshape(256)
    return np.eye(256, dtype=np.float32)[order].astype(ml_dtypes.bfloat16)


def swap_blocks(exchange, read, write, count):
    for first in range(0, count, 2):
        pair = jnp.concatenate(
            [read(first).reshape(256, PIX), read(first + 1).reshape(256, PIX)], axis=1
        )
        moved = jnp.dot(exchange, pair, preferred_element_type=F32).astype(BF16)
        write(first, moved[:, :PIX].reshape(16, 16, PIX))
        write(first + 1, moved[:, PIX:].reshape(16, 16, PIX))


def pack_kernel(half, exchange_ref, *refs):
    about_ref, tile_ref, out_ref = refs if len(refs) == 3 else (None,) + refs
    exchange = exchange_ref[...]
    count = tile_ref.shape[0]
    for start in range(0, count, 16):

        def read(block):
            return tile_ref[start : start + 16, block * 16 : block * 16 + 16, :]

        def write(block, value):
            out_ref[block * 16 : block * 16 + 16, start : start + 16, :] = value

        swap_blocks(exchange, read, write, HALF // 16)
    if about_ref is not None:
        about = about_ref[...]
        for device in range(out_ref.shape[0]):
            out_ref[device, count:, :] = about


def pack(half, exchange, tiles, about=None):
    count = tiles.shape[0]
    extra = 0 if about is None else META
    whole = pl.BlockSpec(memory_space=pltpu.VMEM)
    return pl.pallas_call(
        functools.partial(pack_kernel, half),
        grid=(1,),
        in_specs=[whole] * (1 if about is None else 2)
        + [pl.BlockSpec((count, HALF, PIX), lambda g: (0, half, 0))],
        out_specs=whole,
        out_shape=jax.ShapeDtypeStruct((HALF, count + extra, PIX), BF16),
        compiler_params=pltpu.CompilerParams(vmem_limit_bytes=24 * 1024 * 1024),
        cost_estimate=pl.CostEstimate(
            flops=2 * 256 * count * HALF * PIX, bytes_accessed=4 * count * HALF * PIX, transcendentals=0
        ),
    )(*((exchange, tiles) if about is None else (exchange, about, tiles)))


def coadd_kernel(about_ref, row_ref, coadd_ref, sum_ref):
    sources, count = row_ref.shape[0], about_ref.shape[1] - META
    numbers = lax.broadcasted_iota(jnp.int32, (BINS, PIX), 0).astype(F32)
    ones = jnp.ones((4 * count, PIX), BF16)
    running = jnp.zeros((BINS, 2 * PIX), F32)
    for first in range(0, sources, 4):
        loading = []
        for source in (first, first + 2):
            about = about_ref[source, count:, :].astype(F32) + about_ref[source + 1, count:, :].astype(F32)
            loading.append(jnp.where(about[0:1] == numbers, about[1:2], 0.0).astype(BF16))
        values = jnp.concatenate(
            [row_ref[first : first + 4, 0:count, :].reshape(4 * count, PIX), ones], axis=1
        )
        running = running + jnp.dot(
            jnp.concatenate(loading, axis=1), values, preferred_element_type=F32
        )
    weight_sum = running[:, PIX:]
    coadd_ref[...] = (running[:, :PIX] / jnp.maximum(weight_sum, 1.0)).astype(BF16)
    sum_ref[...] = weight_sum


def coadd_rows(about, rows):
    return pl.pallas_call(
        coadd_kernel,
        out_shape=(
            jax.ShapeDtypeStruct((BINS, PIX), BF16),
            jax.ShapeDtypeStruct((BINS, PIX), F32),
        ),
        compiler_params=pltpu.CompilerParams(vmem_limit_bytes=24 * 1024 * 1024),
        cost_estimate=pl.CostEstimate(
            flops=4 * BINS * 4096 * PIX, bytes_accessed=4 * 4096 * PIX, transcendentals=0
        ),
    )(about, rows)


def detect_kernel(
    place_ref,
    coeff_ref,
    exchange_ref,
    upper_ref,
    lower_ref,
    tile_ref,
    across_ref,
    down_ref,
    smoother_ref,
    out_ref,
    image_ref,
    *scratch,
):
    window_refs, mixed_refs = scratch[:BUFFERS], scratch[BUFFERS:]
    exchange = exchange_ref[...]
    lane = lax.broadcasted_iota(jnp.int32, (SPAN, PIX), 1)
    row = lax.broadcasted_iota(jnp.int32, (SPAN, PIX), 0)
    tile_count = out_ref.shape[0]

    def regroup(block, carry):
        base = pl.multiple_of(block * 16, 16)
        for half, gathered_ref in enumerate((upper_ref, lower_ref)):

            def read(number):
                return gathered_ref[number * 16 : number * 16 + 16, pl.ds(base, 16), :]

            def write(number, value):
                spot = half * HALF + number * 16
                image_ref[pl.ds(base, 16), spot : spot + 16, :] = value

            swap_blocks(exchange, read, write, HALF // 16)
        return carry

    lax.fori_loop(0, BINS // 16, regroup, 0)

    def group(number, window_ref, mixed_ref):
        for local in range(GROUP):
            place = place_ref[number * GROUP + local]
            column = place // 128
            level = place % 128
            other = place + 128 - 256 * column
            outside = ((level == 0) & (row < HALO)) | ((level == 127) & (row >= HALO + PIX))
            wrong_side = (lane // 64) != column
            back = jnp.where(level == 0, 0, 1)
            ahead = jnp.where(level == 127, 0, 1)
            for spot, block, unwanted in ((0, place, outside), (PIX, other, outside | wrong_side)):
                value = jnp.concatenate(
                    [
                        image_ref[block - back, PIX - HALO :, :],
                        image_ref[block],
                        image_ref[block + ahead, 0:HALO, :],
                    ],
                    axis=0,
                )
                value = jnp.where(unwanted, 0.0, value.astype(F32)).astype(BF16)
                window_ref[local * SPAN : (local + 1) * SPAN, spot : spot + PIX] = value
        window = window_ref[...]
        for scale in range(3):
            members = [k for k, pair in enumerate(PAIRS) if pair[0] == scale]
            first, last = members[0], members[-1] + 1
            filtered = jnp.dot(
                window, across_ref[:, first * PIX : last * PIX], preferred_element_type=F32
            )
            for local in range(GROUP):
                rows = slice(local * SPAN, (local + 1) * SPAN)
                base = (number * GROUP + local) * NB
                for power_y in range(DEGREES[scale] + 1):
                    total = None
                    for power_x in range(DEGREES[scale] + 1 - power_y):
                        scalar = coeff_ref[base + BASIS.index((scale, power_x, power_y))]
                        term = scalar * filtered[rows, power_x * PIX : (power_x + 1) * PIX]
                        total = term if total is None else total + term
                    spot = (first + power_y) * SPAN
                    mixed_ref[spot : spot + SPAN, local * PIX : (local + 1) * PIX] = total.astype(BF16)
        begin = pl.multiple_of(number * GROUP, GROUP)
        tiles = tile_ref[pl.ds(begin, GROUP)].reshape(GROUP * PIX, PIX)
        smooth = jnp.dot(tiles, smoother_ref[...], preferred_element_type=F32).astype(BF16)
        spot = len(PAIRS) * SPAN
        for local in range(GROUP):
            mixed_ref[spot : spot + PIX, local * PIX : (local + 1) * PIX] = smooth[
                local * PIX : (local + 1) * PIX
            ]
        result = jnp.dot(down_ref[...], mixed_ref[...], preferred_element_type=F32)
        for local in range(GROUP):
            out_ref[begin + local] = result[:, local * PIX : (local + 1) * PIX].astype(BF16)

    def groups(number, carry):
        for which in range(BUFFERS):
            group(number * BUFFERS + which, window_refs[which], mixed_refs[which])
        return carry

    lax.fori_loop(0, tile_count // (GROUP * BUFFERS), groups, 0)


def detect(place, coeff, exchange, upper, lower, tiles, across, down, smoother):
    tile_count = tiles.shape[0]
    depth = down.shape[1]
    smem = pl.BlockSpec(memory_space=pltpu.SMEM)
    vmem = pl.BlockSpec(memory_space=pltpu.VMEM)
    return pl.pallas_call(
        detect_kernel,
        in_specs=[smem, smem] + [vmem] * 7,
        out_specs=vmem,
        out_shape=jax.ShapeDtypeStruct((tile_count, PIX, PIX), BF16),
        scratch_shapes=[
            pltpu.VMEM((BINS, PIX, PIX), BF16),
        ]
        + [pltpu.VMEM((GROUP * SPAN, 2 * PIX), BF16)] * BUFFERS
        + [pltpu.VMEM((depth, GROUP * PIX), BF16)] * BUFFERS,
        compiler_params=pltpu.CompilerParams(vmem_limit_bytes=48 * 1024 * 1024),
        cost_estimate=pl.CostEstimate(
            flops=2 * tile_count * (SPAN * 256 * 1408 + depth * PIX * PIX),
            bytes_accessed=12 * 1024 * 1024,
            transcendentals=0,
        ),
    )(place, coeff, exchange, upper, lower, tiles, across, down, smoother)


SIDE = 8


def ring_gather(block, row, axis):
    up = [(p, (p + SIDE) % (SIDE * SIDE)) for p in range(SIDE * SIDE)]
    down = [(q, p) for p, q in up]
    result = jnp.zeros((SIDE,) + block.shape, block.dtype)

    def put(array, piece, offset, start=0):
        spot = lax.rem(row + offset + SIDE, SIDE)
        return lax.dynamic_update_slice(array, piece[None], (spot, start) + (0,) * (block.ndim - 1))

    result = put(result, block, 0)
    rising = falling = block
    for step in range(1, SIDE // 2):
        rising, falling = lax.ppermute(rising, axis, up), lax.ppermute(falling, axis, down)
        result = put(put(result, rising, -step), falling, step)
    middle = block.shape[0] // 2
    result = put(result, lax.ppermute(rising[:middle], axis, up), SIDE // 2)
    return put(result, lax.ppermute(falling[middle:], axis, down), SIDE // 2, middle)


def body(visit_tiles, tile_patch, tile_slot, tile_weight, psf_coeff):
    tiles = visit_tiles[0]
    across, down, smoother = (jnp.asarray(m) for m in constants())
    exchange = jnp.asarray(exchange_matrix())
    patch = lax.axis_index("patch")
    place = (tile_slot[0] % 2) * 128 + 2 * tile_patch[0, :, 0] + tile_slot[0] // 2
    facts = jnp.stack([place.astype(F32), tile_weight[0].astype(F32)])
    even = (patch % 2) == 0
    facts = jnp.concatenate([jnp.where(even, facts, 0.0), jnp.where(even, 0.0, facts)], axis=1)
    about = jnp.pad(facts, ((0, META - 2), (0, 0))).astype(BF16)
    coeff = psf_coeff[0].astype(F32).reshape(-1)

    def exchanged(array, groups=None):
        return lax.all_to_all(
            array, "patch", split_axis=0, concat_axis=0, tiled=True, axis_index_groups=groups
        )

    upper_rows = exchanged(pack(0, exchange, tiles, about))
    upper_coadd, weight_sum = coadd_rows(upper_rows, upper_rows)
    lower_packed, upper_coadd = lax.optimization_barrier((pack(1, exchange, tiles), upper_coadd))
    upper = lax.all_gather(upper_coadd, "patch", axis=0, tiled=False)

    lower_coadd, _ = coadd_rows(upper_rows, exchanged(lower_packed))
    along = [[y * SIDE + z for z in range(SIDE)] for y in range(SIDE)]
    lower = exchanged(jnp.broadcast_to(lower_coadd[None], (SIDE,) + lower_coadd.shape), along)
    lower = ring_gather(lower, patch // SIDE, "patch").reshape(SIDE * SIDE, BINS, PIX)

    detection = detect(place, coeff, exchange, upper, lower, tiles, across, down, smoother)

    def own_part(gathered):
        shaped = gathered.reshape(HALF, 2, 128, PIX)
        return lax.dynamic_slice_in_dim(shaped, 2 * patch, 2, axis=2).transpose(2, 0, 1, 3)

    coadd_image = jnp.stack([own_part(upper), own_part(lower)], axis=1)
    own_sum = lax.dynamic_slice_in_dim(weight_sum.reshape(2, 128, PIX), 2 * patch, 2, axis=1)
    own_sum = own_sum.transpose(1, 0, 2)[:, None, None]
    coadd_float = coadd_image.astype(F32)
    terms = (own_sum * coadd_float * coadd_float).reshape(SB * PIX, SB * PIX).astype(BF16)
    terms = lax.all_gather(terms, "band", axis=0, tiled=False)
    chi_image = jnp.sqrt(1.0 + jnp.sum(terms.astype(F32), axis=0)).astype(BF16)
    return (coadd_image.reshape(1, SB * PIX, SB * PIX), detection[None], chi_image)


def solution(mesh):
    return jax.shard_map(
        body,
        mesh=mesh,
        in_specs=(
            P("band", "patch", None, None),
            P("band", "patch", None),
            P("band", "patch"),
            P("band", "patch"),
            P("band", "patch", None),
        ),
        out_specs=(P("band", "patch", None), P("band", "patch", None, None), P("patch", None)),
        check_vma=False,
    )
```

```python
import jax
import jax.numpy as jnp
import ml_dtypes
import numpy as np
from jax import lax
from jax.experimental import pallas as pl
from jax.experimental.pallas import tpu as pltpu
from jax.sharding import PartitionSpec as P

KR = 10
SB = 2
PIX = 128
HALF = 64
HALO = 16
SPAN = PIX + 2 * HALO
META = 16
BINS = 256
GROUP = 4
BUFFERS = 2
NB = 27
SIGMAS = (0.7, 1.5, 3.0)
DEGREES = (4, 2, 2)
BF16 = jnp.bfloat16
F32 = jnp.float32

PAIRS = [(s, p) for s in range(3) for p in range(DEGREES[s] + 1)]
BASIS = [
    (s, i, j)
    for s in range(3)
    for i in range(DEGREES[s] + 1)
    for j in range(DEGREES[s] + 1 - i)
]


def rounded(values):
    return np.asarray(values, np.float32).astype(ml_dtypes.bfloat16)


def kernel_taps(sigma_value, exponent):
    offsets = np.arange(-KR, KR + 1).astype(np.float32)
    gaussian = np.exp(-offsets * offsets / np.float32(2.0 * sigma_value * sigma_value))
    taps = gaussian * (offsets / np.float32(sigma_value)) ** exponent / np.sum(gaussian)
    return rounded(taps).astype(np.float64)


def smooth_taps():
    offsets = np.arange(-KR, KR + 1).astype(np.float32)
    gaussian = np.exp(-offsets * offsets / np.float32(8.0))
    return rounded(gaussian / np.sum(gaussian)).astype(np.float64)


def tap_matrix(taps, source, target):
    distance = source[:, None] - target[None, :]
    inside = np.abs(distance) <= KR
    return np.where(inside, taps[np.clip(distance + KR, 0, 2 * KR)], 0.0)


def constants():
    pixel = np.arange(PIX)
    smoother = tap_matrix(smooth_taps(), pixel, pixel)
    columns = np.concatenate([pixel, PIX + np.arange(64), np.arange(64) - 64])
    across = np.concatenate(
        [tap_matrix(kernel_taps(SIGMAS[s], i), columns, pixel) @ smoother.T for s, i in PAIRS], axis=1
    )
    rows = np.arange(SPAN) - HALO
    down = [-(smoother @ tap_matrix(kernel_taps(SIGMAS[s], j), rows, pixel).T) for s, j in PAIRS]
    return rounded(across), rounded(np.concatenate(down + [smoother], axis=1)), rounded(smoother.T)


def exchange_matrix():
    order = np.arange(256).reshape(16, 16).T.reshape(256)
    return np.eye(256, dtype=np.float32)[order].astype(ml_dtypes.bfloat16)


def swap_blocks(exchange, read, write, count):
    for first in range(0, count, 2):
        pair = jnp.concatenate(
            [read(first).reshape(256, PIX), read(first + 1).reshape(256, PIX)], axis=1
        )
        moved = jnp.dot(exchange, pair, preferred_element_type=F32).astype(BF16)
        write(first, moved[:, :PIX].reshape(16, 16, PIX))
        write(first + 1, moved[:, PIX:].reshape(16, 16, PIX))


def pack_kernel(exchange_ref, about_ref, tile_ref, out_ref):
    exchange = exchange_ref[...]
    count = tile_ref.shape[0]
    for half in range(2):
        for start in range(0, count, 16):

            def read(block):
                spot = half * HALF + block * 16
                return tile_ref[start : start + 16, spot : spot + 16, :]

            def write(block, value):
                spot = half * count + start
                out_ref[block * 16 : block * 16 + 16, spot : spot + 16, :] = value

            swap_blocks(exchange, read, write, HALF // 16)
    about = about_ref[...]
    for device in range(out_ref.shape[0]):
        out_ref[device, 2 * count :, :] = about


def pack(exchange, about, tiles):
    count = tiles.shape[0]
    return pl.pallas_call(
        pack_kernel,
        out_shape=jax.ShapeDtypeStruct((HALF, 2 * count + META, PIX), BF16),
        compiler_params=pltpu.CompilerParams(vmem_limit_bytes=24 * 1024 * 1024),
        cost_estimate=pl.CostEstimate(
            flops=4 * 256 * count * HALF * PIX, bytes_accessed=8 * count * HALF * PIX, transcendentals=0
        ),
    )(exchange, about, tiles)


def coadd_kernel(row_ref, coadd_ref, sum_ref):
    sources = row_ref.shape[0]
    count = (row_ref.shape[1] - META) // 2
    numbers = lax.broadcasted_iota(jnp.int32, (BINS, PIX), 0).astype(F32)
    ones = jnp.ones((4 * count, PIX), BF16)
    running = jnp.zeros((BINS, 3 * PIX), F32)
    for first in range(0, sources, 4):
        loading = []
        for source in (first, first + 2):
            about = row_ref[source, 2 * count :, :].astype(F32) + row_ref[source + 1, 2 * count :, :].astype(F32)
            loading.append(jnp.where(about[0:1] == numbers, about[1:2], 0.0).astype(BF16))
        values = jnp.concatenate(
            [
                row_ref[first : first + 4, 0:count, :].reshape(4 * count, PIX),
                row_ref[first : first + 4, count : 2 * count, :].reshape(4 * count, PIX),
                ones,
            ],
            axis=1,
        )
        running = running + jnp.dot(
            jnp.concatenate(loading, axis=1), values, preferred_element_type=F32
        )
    weight_sum = running[:, 2 * PIX :]
    scale = jnp.maximum(weight_sum, 1.0)
    coadd_ref[0:BINS, :] = (running[:, :PIX] / scale).astype(BF16)
    coadd_ref[BINS:, :] = (running[:, PIX : 2 * PIX] / scale).astype(BF16)
    sum_ref[...] = weight_sum


def coadd_rows(rows):
    return pl.pallas_call(
        coadd_kernel,
        out_shape=(
            jax.ShapeDtypeStruct((2 * BINS, PIX), BF16),
            jax.ShapeDtypeStruct((BINS, PIX), F32),
        ),
        compiler_params=pltpu.CompilerParams(vmem_limit_bytes=24 * 1024 * 1024),
        cost_estimate=pl.CostEstimate(
            flops=6 * BINS * 4096 * PIX, bytes_accessed=4 * 4096 * PIX, transcendentals=0
        ),
    )(rows)


def detect_kernel(
    place_ref,
    coeff_ref,
    exchange_ref,
    gathered_ref,
    tile_ref,
    across_ref,
    down_ref,
    smoother_ref,
    out_ref,
    image_ref,
    *scratch,
):
    window_refs, mixed_refs = scratch[:BUFFERS], scratch[BUFFERS:]
    exchange = exchange_ref[...]
    lane = lax.broadcasted_iota(jnp.int32, (SPAN, PIX), 1)
    row = lax.broadcasted_iota(jnp.int32, (SPAN, PIX), 0)
    tile_count = out_ref.shape[0]

    def regroup(block, carry):
        base = pl.multiple_of(block * 16, 16)
        for half in range(2):

            def read(number):
                start = pl.multiple_of(base + half * BINS, 16)
                return gathered_ref[number * 16 : number * 16 + 16, pl.ds(start, 16), :]

            def write(number, value):
                spot = half * HALF + number * 16
                image_ref[pl.ds(base, 16), spot : spot + 16, :] = value

            swap_blocks(exchange, read, write, HALF // 16)
        return carry

    lax.fori_loop(0, BINS // 16, regroup, 0)

    def group(number, window_ref, mixed_ref):
        for local in range(GROUP):
            place = place_ref[number * GROUP + local]
            column = place // 128
            level = place % 128
            other = place + 128 - 256 * column
            outside = ((level == 0) & (row < HALO)) | ((level == 127) & (row >= HALO + PIX))
            wrong_side = (lane // 64) != column
            back = jnp.where(level == 0, 0, 1)
            ahead = jnp.where(level == 127, 0, 1)
            for spot, block, unwanted in ((0, place, outside), (PIX, other, outside | wrong_side)):
                value = jnp.concatenate(
                    [
                        image_ref[block - back, PIX - HALO :, :],
                        image_ref[block],
                        image_ref[block + ahead, 0:HALO, :],
                    ],
                    axis=0,
                )
                value = jnp.where(unwanted, 0.0, value.astype(F32)).astype(BF16)
                window_ref[local * SPAN : (local + 1) * SPAN, spot : spot + PIX] = value
        window = window_ref[...]
        for scale in range(3):
            members = [k for k, pair in enumerate(PAIRS) if pair[0] == scale]
            first, last = members[0], members[-1] + 1
            filtered = jnp.dot(
                window, across_ref[:, first * PIX : last * PIX], preferred_element_type=F32
            )
            for local in range(GROUP):
                rows = slice(local * SPAN, (local + 1) * SPAN)
                base = (number * GROUP + local) * NB
                for power_y in range(DEGREES[scale] + 1):
                    total = None
                    for power_x in range(DEGREES[scale] + 1 - power_y):
                        scalar = coeff_ref[base + BASIS.index((scale, power_x, power_y))]
                        term = scalar * filtered[rows, power_x * PIX : (power_x + 1) * PIX]
                        total = term if total is None else total + term
                    spot = (first + power_y) * SPAN
                    mixed_ref[spot : spot + SPAN, local * PIX : (local + 1) * PIX] = total.astype(BF16)
        begin = pl.multiple_of(number * GROUP, GROUP)
        tiles = tile_ref[pl.ds(begin, GROUP)].reshape(GROUP * PIX, PIX)
        smooth = jnp.dot(tiles, smoother_ref[...], preferred_element_type=F32).astype(BF16)
        spot = len(PAIRS) * SPAN
        for local in range(GROUP):
            mixed_ref[spot : spot + PIX, local * PIX : (local + 1) * PIX] = smooth[
                local * PIX : (local + 1) * PIX
            ]
        result = jnp.dot(down_ref[...], mixed_ref[...], preferred_element_type=F32)
        for local in range(GROUP):
            out_ref[begin + local] = result[:, local * PIX : (local + 1) * PIX].astype(BF16)

    def groups(number, carry):
        for which in range(BUFFERS):
            group(number * BUFFERS + which, window_refs[which], mixed_refs[which])
        return carry

    lax.fori_loop(0, tile_count // (GROUP * BUFFERS), groups, 0)


def detect(place, coeff, exchange, gathered, tiles, across, down, smoother):
    tile_count = tiles.shape[0]
    depth = down.shape[1]
    smem = pl.BlockSpec(memory_space=pltpu.SMEM)
    vmem = pl.BlockSpec(memory_space=pltpu.VMEM)
    return pl.pallas_call(
        detect_kernel,
        in_specs=[smem, smem] + [vmem] * 6,
        out_specs=vmem,
        out_shape=jax.ShapeDtypeStruct((tile_count, PIX, PIX), BF16),
        scratch_shapes=[
            pltpu.VMEM((BINS, PIX, PIX), BF16),
        ]
        + [pltpu.VMEM((GROUP * SPAN, 2 * PIX), BF16)] * BUFFERS
        + [pltpu.VMEM((depth, GROUP * PIX), BF16)] * BUFFERS,
        compiler_params=pltpu.CompilerParams(vmem_limit_bytes=48 * 1024 * 1024),
        cost_estimate=pl.CostEstimate(
            flops=2 * tile_count * (SPAN * 256 * 1408 + depth * PIX * PIX),
            bytes_accessed=12 * 1024 * 1024,
            transcendentals=0,
        ),
    )(place, coeff, exchange, gathered, tiles, across, down, smoother)


def body(visit_tiles, tile_patch, tile_slot, tile_weight, psf_coeff):
    tiles = visit_tiles[0]
    across, down, smoother = (jnp.asarray(m) for m in constants())
    exchange = jnp.asarray(exchange_matrix())
    patch = lax.axis_index("patch")
    patch_count = lax.axis_size("patch")
    band_count = lax.axis_size("band")
    place = (tile_slot[0] % 2) * 128 + 2 * tile_patch[0, :, 0] + tile_slot[0] // 2
    facts = jnp.stack([place.astype(F32), tile_weight[0].astype(F32)])
    even = (patch % 2) == 0
    facts = jnp.concatenate([jnp.where(even, facts, 0.0), jnp.where(even, 0.0, facts)], axis=1)
    about = jnp.pad(facts, ((0, META - 2), (0, 0))).astype(BF16)
    coeff = psf_coeff[0].astype(F32).reshape(-1)

    def exchanged(array, axis):
        return lax.all_to_all(array, axis, split_axis=0, concat_axis=0, tiled=True)

    rows = exchanged(pack(exchange, about, tiles), "patch")
    coadd, weight_sum = coadd_rows(rows)
    gathered = lax.all_gather(coadd, "patch", axis=0, tiled=False)

    own = coadd.reshape(4, patch_count, 2, PIX).transpose(1, 0, 2, 3).reshape(patch_count, 8, PIX)
    own = exchanged(own, "patch").reshape(HALF, 2, 2, 2, PIX)
    coadd_image = own.transpose(3, 1, 0, 2, 4)
    own_sum = lax.dynamic_slice_in_dim(weight_sum.reshape(2, 128, PIX), 2 * patch, 2, axis=1)
    own_sum = own_sum.transpose(1, 0, 2)[:, None, None]
    coadd_float = coadd_image.astype(F32)
    terms = (own_sum * coadd_float * coadd_float).reshape(SB * PIX, SB * PIX).astype(BF16)
    terms = exchanged(jnp.broadcast_to(terms[None], (band_count,) + terms.shape), "band")
    chi_image = jnp.sqrt(1.0 + jnp.sum(terms.astype(F32), axis=0)).astype(BF16)
    coadd_image = coadd_image.reshape(1, SB * PIX, SB * PIX)

    gathered, chi_image, coadd_image = lax.optimization_barrier((gathered, chi_image, coadd_image))
    detection = detect(place, coeff, exchange, gathered, tiles, across, down, smoother)
    return (coadd_image, detection[None], chi_image)


def solution(mesh):
    return jax.shard_map(
        body,
        mesh=mesh,
        in_specs=(
            P("band", "patch", None, None),
            P("band", "patch", None),
            P("band", "patch"),
            P("band", "patch"),
            P("band", "patch", None),
        ),
        out_specs=(P("band", "patch", None), P("band", "patch", None, None), P("patch", None)),
        check_vma=False,
    )
```

```python
import functools

import jax
import jax.numpy as jnp
import ml_dtypes
import numpy as np
from jax import lax
from jax.experimental import pallas as pl
from jax.experimental.pallas import tpu as pltpu
from jax.sharding import PartitionSpec as P

KR = 10
SB = 2
PIX = 128
HALF = 64
HALO = 16
SPAN = PIX + 2 * HALO
META = 16
BINS = 256
GROUP = 4
BUFFERS = 2
NB = 27
SIGMAS = (0.7, 1.5, 3.0)
DEGREES = (4, 2, 2)
BF16 = jnp.bfloat16
F32 = jnp.float32

PAIRS = [(s, p) for s in range(3) for p in range(DEGREES[s] + 1)]
BASIS = [
    (s, i, j)
    for s in range(3)
    for i in range(DEGREES[s] + 1)
    for j in range(DEGREES[s] + 1 - i)
]


def rounded(values):
    return np.asarray(values, np.float32).astype(ml_dtypes.bfloat16)


def kernel_taps(sigma_value, exponent):
    offsets = np.arange(-KR, KR + 1).astype(np.float32)
    gaussian = np.exp(-offsets * offsets / np.float32(2.0 * sigma_value * sigma_value))
    taps = gaussian * (offsets / np.float32(sigma_value)) ** exponent / np.sum(gaussian)
    return rounded(taps).astype(np.float64)


def smooth_taps():
    offsets = np.arange(-KR, KR + 1).astype(np.float32)
    gaussian = np.exp(-offsets * offsets / np.float32(8.0))
    return rounded(gaussian / np.sum(gaussian)).astype(np.float64)


def tap_matrix(taps, source, target):
    distance = source[:, None] - target[None, :]
    inside = np.abs(distance) <= KR
    return np.where(inside, taps[np.clip(distance + KR, 0, 2 * KR)], 0.0)


def constants():
    pixel = np.arange(PIX)
    smoother = tap_matrix(smooth_taps(), pixel, pixel)
    columns = np.concatenate([pixel, PIX + np.arange(64), np.arange(64) - 64])
    across = np.concatenate(
        [tap_matrix(kernel_taps(SIGMAS[s], i), columns, pixel) @ smoother.T for s, i in PAIRS], axis=1
    )
    rows = np.arange(SPAN) - HALO
    down = [-(smoother @ tap_matrix(kernel_taps(SIGMAS[s], j), rows, pixel).T) for s, j in PAIRS]
    return rounded(across), rounded(np.concatenate(down + [smoother], axis=1)), rounded(smoother.T)


def exchange_matrix():
    order = np.arange(256).reshape(16, 16).T.reshape(256)
    return np.eye(256, dtype=np.float32)[order].astype(ml_dtypes.bfloat16)


def swap_blocks(exchange, read, write, count):
    for first in range(0, count, 2):
        pair = jnp.concatenate(
            [read(first).reshape(256, PIX), read(first + 1).reshape(256, PIX)], axis=1
        )
        moved = jnp.dot(exchange, pair, preferred_element_type=F32).astype(BF16)
        write(first, moved[:, :PIX].reshape(16, 16, PIX))
        write(first + 1, moved[:, PIX:].reshape(16, 16, PIX))


def pack_kernel(exchange_ref, about_ref, tile_ref, out_ref):
    exchange = exchange_ref[...]
    count = tile_ref.shape[0]
    for half in range(2):
        for start in range(0, count, 16):

            def read(block):
                spot = half * HALF + block * 16
                return tile_ref[start : start + 16, spot : spot + 16, :]

            def write(block, value):
                spot = half * count + start
                out_ref[block * 16 : block * 16 + 16, spot : spot + 16, :] = value

            swap_blocks(exchange, read, write, HALF // 16)
    about = about_ref[...]
    for device in range(out_ref.shape[0]):
        out_ref[device, 2 * count :, :] = about


def pack(exchange, about, tiles):
    count = tiles.shape[0]
    return pl.pallas_call(
        pack_kernel,
        out_shape=jax.ShapeDtypeStruct((HALF, 2 * count + META, PIX), BF16),
        compiler_params=pltpu.CompilerParams(vmem_limit_bytes=24 * 1024 * 1024),
        cost_estimate=pl.CostEstimate(
            flops=4 * 256 * count * HALF * PIX, bytes_accessed=8 * count * HALF * PIX, transcendentals=0
        ),
    )(exchange, about, tiles)


def coadd_kernel(row_ref, coadd_ref, sum_ref):
    sources = row_ref.shape[0]
    count = (row_ref.shape[1] - META) // 2
    numbers = lax.broadcasted_iota(jnp.int32, (BINS, PIX), 0).astype(F32)
    ones = jnp.ones((4 * count, PIX), BF16)
    running = jnp.zeros((BINS, 3 * PIX), F32)
    for first in range(0, sources, 4):
        loading = []
        for source in (first, first + 2):
            about = row_ref[source, 2 * count :, :].astype(F32) + row_ref[source + 1, 2 * count :, :].astype(F32)
            loading.append(jnp.where(about[0:1] == numbers, about[1:2], 0.0).astype(BF16))
        values = jnp.concatenate(
            [
                row_ref[first : first + 4, 0:count, :].reshape(4 * count, PIX),
                row_ref[first : first + 4, count : 2 * count, :].reshape(4 * count, PIX),
                ones,
            ],
            axis=1,
        )
        running = running + jnp.dot(
            jnp.concatenate(loading, axis=1), values, preferred_element_type=F32
        )
    weight_sum = running[:, 2 * PIX :]
    scale = jnp.maximum(weight_sum, 1.0)
    coadd_ref[0:BINS, :] = (running[:, :PIX] / scale).astype(BF16)
    coadd_ref[BINS:, :] = (running[:, PIX : 2 * PIX] / scale).astype(BF16)
    sum_ref[...] = weight_sum


def coadd_rows(rows):
    return pl.pallas_call(
        coadd_kernel,
        out_shape=(
            jax.ShapeDtypeStruct((2 * BINS, PIX), BF16),
            jax.ShapeDtypeStruct((BINS, PIX), F32),
        ),
        compiler_params=pltpu.CompilerParams(vmem_limit_bytes=24 * 1024 * 1024),
        cost_estimate=pl.CostEstimate(
            flops=6 * BINS * 4096 * PIX, bytes_accessed=4 * 4096 * PIX, transcendentals=0
        ),
    )(rows)


def detect_kernel(
    place_ref,
    coeff_ref,
    exchange_ref,
    gathered_ref,
    tile_source,
    across_source,
    down_source,
    smoother_ref,
    out_ref,
    image_ref,
    held_ref,
    tile_ref,
    across_ref,
    down_ref,
    arrived,
    *scratch,
):
    window_refs, mixed_refs = scratch[:BUFFERS], scratch[BUFFERS:]

    def piece(part):
        spot = pl.ds(part * 16, 16)
        return pltpu.make_async_copy(gathered_ref.at[spot], held_ref.at[spot], arrived.at[part])

    others = [
        pltpu.make_async_copy(source, target, arrived.at[HALF // 16 + number])
        for number, (source, target) in enumerate(
            ((tile_source, tile_ref), (across_source, across_ref), (down_source, down_ref))
        )
    ]
    for part in range(HALF // 16):
        piece(part).start()
    for other in others:
        other.start()
    exchange = exchange_ref[...]
    lane = lax.broadcasted_iota(jnp.int32, (SPAN, PIX), 1)
    row = lax.broadcasted_iota(jnp.int32, (SPAN, PIX), 0)
    tile_count = out_ref.shape[0]

    def regroup(part, block, carry):
        base = pl.multiple_of(block * 16, 16)

        def read(half):
            start = pl.multiple_of(base + half * BINS, 16)
            return held_ref[part * 16 : part * 16 + 16, pl.ds(start, 16), :]

        def write(half, value):
            spot = half * HALF + part * 16
            image_ref[pl.ds(base, 16), spot : spot + 16, :] = value

        swap_blocks(exchange, read, write, 2)
        return carry

    for part in range(HALF // 16):
        piece(part).wait()
        lax.fori_loop(0, BINS // 16, functools.partial(regroup, part), 0, unroll=16)

    for other in others:
        other.wait()

    def group(number, window_ref, mixed_ref):
        for local in range(GROUP):
            place = place_ref[number * GROUP + local]
            column = place // 128
            level = place % 128
            other = place + 128 - 256 * column
            outside = ((level == 0) & (row < HALO)) | ((level == 127) & (row >= HALO + PIX))
            wrong_side = (lane // 64) != column
            back = jnp.where(level == 0, 0, 1)
            ahead = jnp.where(level == 127, 0, 1)
            for spot, block, unwanted in ((0, place, outside), (PIX, other, outside | wrong_side)):
                value = jnp.concatenate(
                    [
                        image_ref[block - back, PIX - HALO :, :],
                        image_ref[block],
                        image_ref[block + ahead, 0:HALO, :],
                    ],
                    axis=0,
                )
                value = jnp.where(unwanted, 0.0, value.astype(F32)).astype(BF16)
                window_ref[local * SPAN : (local + 1) * SPAN, spot : spot + PIX] = value
        window = window_ref[...]
        for scale in range(3):
            members = [k for k, pair in enumerate(PAIRS) if pair[0] == scale]
            first, last = members[0], members[-1] + 1
            filtered = jnp.dot(
                window, across_ref[:, first * PIX : last * PIX], preferred_element_type=F32
            )
            for local in range(GROUP):
                rows = slice(local * SPAN, (local + 1) * SPAN)
                base = (number * GROUP + local) * NB
                for power_y in range(DEGREES[scale] + 1):
                    total = None
                    for power_x in range(DEGREES[scale] + 1 - power_y):
                        scalar = coeff_ref[base + BASIS.index((scale, power_x, power_y))]
                        term = scalar * filtered[rows, power_x * PIX : (power_x + 1) * PIX]
                        total = term if total is None else total + term
                    spot = (first + power_y) * SPAN
                    mixed_ref[spot : spot + SPAN, local * PIX : (local + 1) * PIX] = total.astype(BF16)
        begin = pl.multiple_of(number * GROUP, GROUP)
        tiles = tile_ref[pl.ds(begin, GROUP)].reshape(GROUP * PIX, PIX)
        smooth = jnp.dot(tiles, smoother_ref[...], preferred_element_type=F32).astype(BF16)
        spot = len(PAIRS) * SPAN
        for local in range(GROUP):
            mixed_ref[spot : spot + PIX, local * PIX : (local + 1) * PIX] = smooth[
                local * PIX : (local + 1) * PIX
            ]
        result = jnp.dot(down_ref[...], mixed_ref[...], preferred_element_type=F32)
        for local in range(GROUP):
            out_ref[begin + local] = result[:, local * PIX : (local + 1) * PIX].astype(BF16)

    def groups(number, carry):
        for which in range(BUFFERS):
            group(number * BUFFERS + which, window_refs[which], mixed_refs[which])
        return carry

    lax.fori_loop(0, tile_count // (GROUP * BUFFERS), groups, 0)


def detect(place, coeff, exchange, gathered, tiles, across, down, smoother):
    tile_count = tiles.shape[0]
    depth = down.shape[1]
    smem = pl.BlockSpec(memory_space=pltpu.SMEM)
    vmem = pl.BlockSpec(memory_space=pltpu.VMEM)
    return pl.pallas_call(
        detect_kernel,
        in_specs=[smem, smem, vmem] + [pl.BlockSpec(memory_space=pl.ANY)] * 4 + [vmem],
        out_specs=vmem,
        out_shape=jax.ShapeDtypeStruct((tile_count, PIX, PIX), BF16),
        scratch_shapes=[
            pltpu.VMEM((BINS, PIX, PIX), BF16),
            pltpu.VMEM(gathered.shape, BF16),
            pltpu.VMEM(tiles.shape, BF16),
            pltpu.VMEM(across.shape, BF16),
            pltpu.VMEM(down.shape, BF16),
            pltpu.SemaphoreType.DMA((HALF // 16 + 3,)),
        ]
        + [pltpu.VMEM((GROUP * SPAN, 2 * PIX), BF16)] * BUFFERS
        + [pltpu.VMEM((depth, GROUP * PIX), BF16)] * BUFFERS,
        compiler_params=pltpu.CompilerParams(vmem_limit_bytes=48 * 1024 * 1024),
        cost_estimate=pl.CostEstimate(
            flops=2 * tile_count * (SPAN * 256 * 1408 + depth * PIX * PIX),
            bytes_accessed=12 * 1024 * 1024,
            transcendentals=0,
        ),
    )(place, coeff, exchange, gathered, tiles, across, down, smoother)


def body(visit_tiles, tile_patch, tile_slot, tile_weight, psf_coeff):
    tiles = visit_tiles[0]
    across, down, smoother = (jnp.asarray(m) for m in constants())
    exchange = jnp.asarray(exchange_matrix())
    patch = lax.axis_index("patch")
    patch_count = lax.axis_size("patch")
    band_count = lax.axis_size("band")
    place = (tile_slot[0] % 2) * 128 + 2 * tile_patch[0, :, 0] + tile_slot[0] // 2
    facts = jnp.stack([place.astype(F32), tile_weight[0].astype(F32)])
    even = (patch % 2) == 0
    facts = jnp.concatenate([jnp.where(even, facts, 0.0), jnp.where(even, 0.0, facts)], axis=1)
    about = jnp.pad(facts, ((0, META - 2), (0, 0))).astype(BF16)
    coeff = psf_coeff[0].astype(F32).reshape(-1)

    def exchanged(array, axis):
        return lax.all_to_all(array, axis, split_axis=0, concat_axis=0, tiled=True)

    rows = exchanged(pack(exchange, about, tiles), "patch")
    coadd, weight_sum = coadd_rows(rows)
    gathered = lax.all_gather(coadd, "patch", axis=0, tiled=False)

    own = coadd.reshape(4, patch_count, 2, PIX).transpose(1, 0, 2, 3).reshape(patch_count, 8, PIX)
    own = exchanged(own, "patch").reshape(HALF, 2, 2, 2, PIX)
    coadd_image = own.transpose(3, 1, 0, 2, 4)
    own_sum = lax.dynamic_slice_in_dim(weight_sum.reshape(2, 128, PIX), 2 * patch, 2, axis=1)
    own_sum = own_sum.transpose(1, 0, 2)[:, None, None]
    coadd_float = coadd_image.astype(F32)
    terms = (own_sum * coadd_float * coadd_float).reshape(SB * PIX, SB * PIX).astype(BF16)
    terms = exchanged(jnp.broadcast_to(terms[None], (band_count,) + terms.shape), "band")
    chi_image = jnp.sqrt(1.0 + jnp.sum(terms.astype(F32), axis=0)).astype(BF16)
    coadd_image = coadd_image.reshape(1, SB * PIX, SB * PIX)

    gathered, chi_image, coadd_image = lax.optimization_barrier((gathered, chi_image, coadd_image))
    detection = detect(place, coeff, exchange, gathered, tiles, across, down, smoother)
    return (coadd_image, detection[None], chi_image)


def solution(mesh):
    return jax.shard_map(
        body,
        mesh=mesh,
        in_specs=(
            P("band", "patch", None, None),
            P("band", "patch", None),
            P("band", "patch"),
            P("band", "patch"),
            P("band", "patch", None),
        ),
        out_specs=(P("band", "patch", None), P("band", "patch", None, None), P("patch", None)),
        check_vma=False,
    )
```

```python
import functools

import jax
import jax.numpy as jnp
import ml_dtypes
import numpy as np
from jax import lax
from jax.experimental import pallas as pl
from jax.experimental.pallas import tpu as pltpu
from jax.sharding import PartitionSpec as P

KR = 10
SB = 2
PIX = 128
HALF = 64
HALO = 16
SPAN = PIX + 2 * HALO
META = 16
BINS = 256
GROUP = 4
BUFFERS = 2
NB = 27
SIGMAS = (0.7, 1.5, 3.0)
DEGREES = (4, 2, 2)
BF16 = jnp.bfloat16
F32 = jnp.float32

PAIRS = [(s, p) for s in range(3) for p in range(DEGREES[s] + 1)]
BASIS = [
    (s, i, j)
    for s in range(3)
    for i in range(DEGREES[s] + 1)
    for j in range(DEGREES[s] + 1 - i)
]


def rounded(values):
    return np.asarray(values, np.float32).astype(ml_dtypes.bfloat16)


def kernel_taps(sigma_value, exponent):
    offsets = np.arange(-KR, KR + 1).astype(np.float32)
    gaussian = np.exp(-offsets * offsets / np.float32(2.0 * sigma_value * sigma_value))
    taps = gaussian * (offsets / np.float32(sigma_value)) ** exponent / np.sum(gaussian)
    return rounded(taps).astype(np.float64)


def smooth_taps():
    offsets = np.arange(-KR, KR + 1).astype(np.float32)
    gaussian = np.exp(-offsets * offsets / np.float32(8.0))
    return rounded(gaussian / np.sum(gaussian)).astype(np.float64)


def tap_matrix(taps, source, target):
    distance = source[:, None] - target[None, :]
    inside = np.abs(distance) <= KR
    return np.where(inside, taps[np.clip(distance + KR, 0, 2 * KR)], 0.0)


def constants():
    pixel = np.arange(PIX)
    smoother = tap_matrix(smooth_taps(), pixel, pixel)
    columns = np.concatenate([pixel, PIX + np.arange(64), np.arange(64) - 64])
    across = np.concatenate(
        [tap_matrix(kernel_taps(SIGMAS[s], i), columns, pixel) @ smoother.T for s, i in PAIRS], axis=1
    )
    rows = np.arange(SPAN) - HALO
    down = [-(smoother @ tap_matrix(kernel_taps(SIGMAS[s], j), rows, pixel).T) for s, j in PAIRS]
    return rounded(across), rounded(np.concatenate(down, axis=1)), rounded(smoother.T)


def exchange_matrix():
    row = lax.broadcasted_iota(jnp.int32, (256, 256), 0)
    column = lax.broadcasted_iota(jnp.int32, (256, 256), 1)
    return jnp.where(column == (row % 16) * 16 + row // 16, 1.0, 0.0).astype(BF16)


def swap_blocks(exchange, read, write, count):
    for first in range(0, count, 2):
        pair = jnp.concatenate(
            [read(first).reshape(256, PIX), read(first + 1).reshape(256, PIX)], axis=1
        )
        moved = jnp.dot(exchange, pair, preferred_element_type=F32).astype(BF16)
        write(first, moved[:, :PIX].reshape(16, 16, PIX))
        write(first + 1, moved[:, PIX:].reshape(16, 16, PIX))


def block_number(patch, slot):
    return (slot & 1) * 128 + 2 * patch + (slot >> 1)


def pack_kernel(patch_ref, slot_ref, weight_ref, tile_ref, out_ref):
    exchange = exchange_matrix()
    count = tile_ref.shape[0]
    for half in range(2):
        for start in range(0, count, 16):

            def read(block):
                spot = half * HALF + block * 16
                return tile_ref[start : start + 16, spot : spot + 16, :]

            def write(block, value):
                spot = half * count + start
                out_ref[block * 16 : block * 16 + 16, spot : spot + 16, :] = value

            swap_blocks(exchange, read, write, HALF // 16)
    number = block_number(patch_ref[...], slot_ref[...]).astype(F32)
    weight = weight_ref[...].astype(F32)
    number = jnp.concatenate([number, number], axis=1)
    weight = jnp.concatenate([weight, weight], axis=1)
    row = lax.broadcasted_iota(jnp.int32, (META, PIX), 0)
    about = jnp.where(row == 0, number, jnp.where(row == 1, weight, 0.0)).astype(BF16)
    for device in range(out_ref.shape[0]):
        out_ref[device, 2 * count :, :] = about


def pack(patch, slot, weight, tiles):
    count = tiles.shape[0]
    return pl.pallas_call(
        pack_kernel,
        out_shape=jax.ShapeDtypeStruct((HALF, 2 * count + META, PIX), BF16),
        compiler_params=pltpu.CompilerParams(vmem_limit_bytes=24 * 1024 * 1024),
        cost_estimate=pl.CostEstimate(
            flops=4 * 256 * count * HALF * PIX, bytes_accessed=8 * count * HALF * PIX, transcendentals=0
        ),
    )(patch, slot, weight, tiles)


def smooth_kernel(tile_ref, smoother_ref, out_ref):
    smoother = smoother_ref[...]
    across = jnp.dot(
        tile_ref[...].reshape(-1, PIX), smoother, preferred_element_type=F32
    ).astype(BF16)
    for tile in range(tile_ref.shape[0]):
        out_ref[tile] = lax.dot_general(
            smoother,
            across[tile * PIX : (tile + 1) * PIX],
            (((0,), (0,)), ((), ())),
            preferred_element_type=F32,
        )


def smooth_tiles(tiles, smoother):
    count = tiles.shape[0]
    return pl.pallas_call(
        smooth_kernel,
        grid=(count // 8,),
        in_specs=[
            pl.BlockSpec((8, PIX, PIX), lambda g: (g, 0, 0)),
            pl.BlockSpec((PIX, PIX), lambda g: (0, 0)),
        ],
        out_specs=pl.BlockSpec((8, PIX, PIX), lambda g: (g, 0, 0)),
        out_shape=jax.ShapeDtypeStruct(tiles.shape, F32),
        cost_estimate=pl.CostEstimate(
            flops=4 * count * PIX**3, bytes_accessed=6 * count * PIX * PIX, transcendentals=0
        ),
    )(tiles, smoother)


def coadd_kernel(row_ref, coadd_ref, sum_ref):
    sources = row_ref.shape[0]
    count = (row_ref.shape[1] - META) // 2
    numbers = lax.broadcasted_iota(jnp.int32, (BINS, PIX), 0).astype(F32)
    first_source = lax.broadcasted_iota(jnp.int32, (META, PIX), 1) < count
    ones = jnp.ones((4 * count, PIX), BF16)
    running = jnp.zeros((BINS, 3 * PIX), F32)
    for first in range(0, sources, 4):
        loading = []
        for source in (first, first + 2):
            about = jnp.where(
                first_source,
                row_ref[source, 2 * count :, :].astype(F32),
                row_ref[source + 1, 2 * count :, :].astype(F32),
            )
            loading.append(jnp.where(about[0:1] == numbers, about[1:2], 0.0).astype(BF16))
        values = jnp.concatenate(
            [
                row_ref[first : first + 4, 0:count, :].reshape(4 * count, PIX),
                row_ref[first : first + 4, count : 2 * count, :].reshape(4 * count, PIX),
                ones,
            ],
            axis=1,
        )
        running = running + jnp.dot(
            jnp.concatenate(loading, axis=1), values, preferred_element_type=F32
        )
    weight_sum = running[:, 2 * PIX :]
    scale = jnp.maximum(weight_sum, 1.0)
    coadd_ref[0:BINS, :] = (running[:, :PIX] / scale).astype(BF16)
    coadd_ref[BINS:, :] = (running[:, PIX : 2 * PIX] / scale).astype(BF16)
    sum_ref[...] = weight_sum


def coadd_rows(rows):
    return pl.pallas_call(
        coadd_kernel,
        out_shape=(
            jax.ShapeDtypeStruct((2 * BINS, PIX), BF16),
            jax.ShapeDtypeStruct((BINS, PIX), F32),
        ),
        compiler_params=pltpu.CompilerParams(vmem_limit_bytes=24 * 1024 * 1024),
        cost_estimate=pl.CostEstimate(
            flops=6 * BINS * 4096 * PIX, bytes_accessed=4 * 4096 * PIX, transcendentals=0
        ),
    )(rows)


def detect_kernel(
    place_ref,
    coeff_ref,
    gathered_ref,
    tile_source,
    across_source,
    down_source,
    out_ref,
    image_ref,
    held_ref,
    tile_ref,
    across_ref,
    down_ref,
    arrived,
    *scratch,
):
    window_refs, mixed_refs = scratch[:BUFFERS], scratch[BUFFERS:]

    def piece(part):
        spot = pl.ds(part * 16, 16)
        return pltpu.make_async_copy(gathered_ref.at[spot], held_ref.at[spot], arrived.at[part])

    others = [
        pltpu.make_async_copy(source, target, arrived.at[HALF // 16 + number])
        for number, (source, target) in enumerate(
            ((tile_source, tile_ref), (across_source, across_ref), (down_source, down_ref))
        )
    ]
    for part in range(HALF // 16):
        piece(part).start()
    for other in others:
        other.start()
    exchange = exchange_matrix()
    lane = lax.broadcasted_iota(jnp.int32, (SPAN, PIX), 1)
    row = lax.broadcasted_iota(jnp.int32, (SPAN, PIX), 0)
    tile_count = out_ref.shape[0]

    def regroup(part, block, carry):
        base = pl.multiple_of(block * 16, 16)

        def read(half):
            start = pl.multiple_of(base + half * BINS, 16)
            return held_ref[part * 16 : part * 16 + 16, pl.ds(start, 16), :]

        def write(half, value):
            spot = half * HALF + part * 16
            image_ref[pl.ds(base, 16), spot : spot + 16, :] = value

        swap_blocks(exchange, read, write, 2)
        return carry

    for part in range(HALF // 16):
        piece(part).wait()
        lax.fori_loop(0, BINS // 16, functools.partial(regroup, part), 0, unroll=16)

    for other in others:
        other.wait()

    def group(number, window_ref, mixed_ref):
        for local in range(GROUP):
            place = place_ref[number * GROUP + local]
            column = place // 128
            level = place % 128
            other = place + 128 - 256 * column
            outside = ((level == 0) & (row < HALO)) | ((level == 127) & (row >= HALO + PIX))
            wrong_side = (lane // 64) != column
            back = jnp.where(level == 0, 0, 1)
            ahead = jnp.where(level == 127, 0, 1)
            for spot, block, unwanted in ((0, place, outside), (PIX, other, outside | wrong_side)):
                value = jnp.concatenate(
                    [
                        image_ref[block - back, PIX - HALO :, :],
                        image_ref[block],
                        image_ref[block + ahead, 0:HALO, :],
                    ],
                    axis=0,
                )
                value = jnp.where(unwanted, 0.0, value.astype(F32)).astype(BF16)
                window_ref[local * SPAN : (local + 1) * SPAN, spot : spot + PIX] = value
        window = window_ref[...]
        for scale in range(3):
            members = [k for k, pair in enumerate(PAIRS) if pair[0] == scale]
            first, last = members[0], members[-1] + 1
            filtered = jnp.dot(
                window, across_ref[:, first * PIX : last * PIX], preferred_element_type=F32
            )
            for local in range(GROUP):
                rows = slice(local * SPAN, (local + 1) * SPAN)
                base = (number * GROUP + local) * NB
                for power_y in range(DEGREES[scale] + 1):
                    total = None
                    for power_x in range(DEGREES[scale] + 1 - power_y):
                        scalar = coeff_ref[base + BASIS.index((scale, power_x, power_y))]
                        term = scalar * filtered[rows, power_x * PIX : (power_x + 1) * PIX]
                        total = term if total is None else total + term
                    spot = (first + power_y) * SPAN
                    mixed_ref[spot : spot + SPAN, local * PIX : (local + 1) * PIX] = total.astype(BF16)
        begin = pl.multiple_of(number * GROUP, GROUP)
        result = jnp.dot(down_ref[...], mixed_ref[...], preferred_element_type=F32)
        for local in range(GROUP):
            piece = result[:, local * PIX : (local + 1) * PIX] + tile_ref[begin + local]
            out_ref[begin + local] = piece.astype(BF16)

    def groups(number, carry):
        for which in range(BUFFERS):
            group(number * BUFFERS + which, window_refs[which], mixed_refs[which])
        return carry

    lax.fori_loop(0, tile_count // (GROUP * BUFFERS), groups, 0)


def detect(place, coeff, gathered, tiles, across, down):
    tile_count = tiles.shape[0]
    depth = down.shape[1]
    smem = pl.BlockSpec(memory_space=pltpu.SMEM)
    vmem = pl.BlockSpec(memory_space=pltpu.VMEM)
    return pl.pallas_call(
        detect_kernel,
        in_specs=[smem, smem] + [pl.BlockSpec(memory_space=pl.ANY)] * 4,
        out_specs=vmem,
        out_shape=jax.ShapeDtypeStruct((tile_count, PIX, PIX), BF16),
        scratch_shapes=[
            pltpu.VMEM((BINS, PIX, PIX), BF16),
            pltpu.VMEM(gathered.shape, BF16),
            pltpu.VMEM(tiles.shape, F32),
            pltpu.VMEM(across.shape, BF16),
            pltpu.VMEM(down.shape, BF16),
            pltpu.SemaphoreType.DMA((HALF // 16 + 3,)),
        ]
        + [pltpu.VMEM((GROUP * SPAN, 2 * PIX), BF16)] * BUFFERS
        + [pltpu.VMEM((depth, GROUP * PIX), BF16)] * BUFFERS,
        compiler_params=pltpu.CompilerParams(vmem_limit_bytes=48 * 1024 * 1024),
        cost_estimate=pl.CostEstimate(
            flops=2 * tile_count * (SPAN * 256 * 1408 + depth * PIX * PIX),
            bytes_accessed=12 * 1024 * 1024,
            transcendentals=0,
        ),
    )(place, coeff, gathered, tiles, across, down)


def body(visit_tiles, tile_patch, tile_slot, tile_weight, psf_coeff):
    tiles = visit_tiles[0]
    across, down, smoother = (jnp.asarray(m) for m in constants())
    patch = lax.axis_index("patch")
    patch_count = lax.axis_size("patch")
    band_count = lax.axis_size("band")
    tile_patch = tile_patch.reshape(tile_slot.shape)
    place = block_number(tile_patch[0], tile_slot[0])
    coeff = psf_coeff[0].astype(F32).reshape(-1)

    def exchanged(array, axis):
        return lax.all_to_all(array, axis, split_axis=0, concat_axis=0, tiled=True)

    rows = exchanged(pack(tile_patch, tile_slot, tile_weight, tiles), "patch")
    coadd, weight_sum = coadd_rows(rows)
    gathered = lax.all_gather(coadd, "patch", axis=0, tiled=False)

    own = coadd.reshape(4, patch_count, 2, PIX).transpose(1, 0, 2, 3).reshape(patch_count, 8, PIX)
    own = exchanged(own, "patch").reshape(HALF, 2, 2, 2, PIX)
    coadd_image = own.transpose(3, 1, 0, 2, 4)
    own_sum = lax.dynamic_slice_in_dim(weight_sum.reshape(2, 128, PIX), 2 * patch, 2, axis=1)
    own_sum = own_sum.transpose(1, 0, 2)[:, None, None]
    coadd_float = coadd_image.astype(F32)
    terms = (own_sum * coadd_float * coadd_float).reshape(SB * PIX, SB * PIX).astype(BF16)
    terms = exchanged(jnp.broadcast_to(terms[None], (band_count,) + terms.shape), "band")
    chi_image = jnp.sqrt(1.0 + jnp.sum(terms.astype(F32), axis=0)).astype(BF16)
    coadd_image = coadd_image.reshape(1, SB * PIX, SB * PIX)

    later, coadd = lax.optimization_barrier((tiles, coadd))
    smoothed = smooth_tiles(later, smoother)
    gathered, smoothed, chi_image, coadd_image = lax.optimization_barrier(
        (gathered, smoothed, chi_image, coadd_image)
    )
    detection = detect(place, coeff, gathered, smoothed, across, down)
    return (coadd_image, detection[None], chi_image)


def solution(mesh):
    return jax.shard_map(
        body,
        mesh=mesh,
        in_specs=(
            P("band", "patch", None, None),
            P("band", "patch", None),
            P("band", "patch"),
            P("band", "patch"),
            P("band", "patch", None),
        ),
        out_specs=(P("band", "patch", None), P("band", "patch", None, None), P("patch", None)),
        check_vma=False,
    )
```

```python
import functools

import jax
import jax.numpy as jnp
import ml_dtypes
import numpy as np
from jax import lax
from jax.experimental import pallas as pl
from jax.experimental.pallas import tpu as pltpu
from jax.sharding import PartitionSpec as P

KR = 10
SB = 2
PIX = 128
HALF = 64
HALO = 16
SPAN = PIX + 2 * HALO
META = 16
BINS = 256
GROUP = 4
BUFFERS = 2
NB = 27
SIGMAS = (0.7, 1.5, 3.0)
DEGREES = (4, 2, 2)
BF16 = jnp.bfloat16
F32 = jnp.float32

PAIRS = [(s, p) for s in range(3) for p in range(DEGREES[s] + 1)]
BASIS = [
    (s, i, j)
    for s in range(3)
    for i in range(DEGREES[s] + 1)
    for j in range(DEGREES[s] + 1 - i)
]


def rounded(values):
    return np.asarray(values, np.float32).astype(ml_dtypes.bfloat16)


def kernel_taps(sigma_value, exponent):
    offsets = np.arange(-KR, KR + 1).astype(np.float32)
    gaussian = np.exp(-offsets * offsets / np.float32(2.0 * sigma_value * sigma_value))
    taps = gaussian * (offsets / np.float32(sigma_value)) ** exponent / np.sum(gaussian)
    return rounded(taps).astype(np.float64)


def smooth_taps():
    offsets = np.arange(-KR, KR + 1).astype(np.float32)
    gaussian = np.exp(-offsets * offsets / np.float32(8.0))
    return rounded(gaussian / np.sum(gaussian)).astype(np.float64)


def tap_matrix(taps, source, target):
    distance = source[:, None] - target[None, :]
    inside = np.abs(distance) <= KR
    return np.where(inside, taps[np.clip(distance + KR, 0, 2 * KR)], 0.0)


def constants():
    pixel = np.arange(PIX)
    smoother = tap_matrix(smooth_taps(), pixel, pixel)
    columns = np.concatenate([pixel, PIX + np.arange(64), np.arange(64) - 64])
    across = np.concatenate(
        [tap_matrix(kernel_taps(SIGMAS[s], i), columns, pixel) @ smoother.T for s, i in PAIRS], axis=1
    )
    rows = np.arange(SPAN) - HALO
    down = [-(smoother @ tap_matrix(kernel_taps(SIGMAS[s], j), rows, pixel).T) for s, j in PAIRS]
    return rounded(across), rounded(np.concatenate(down, axis=1)), rounded(smoother.T)


def exchange_matrix():
    row = lax.broadcasted_iota(jnp.int32, (256, 256), 0)
    column = lax.broadcasted_iota(jnp.int32, (256, 256), 1)
    return jnp.where(column == (row % 16) * 16 + row // 16, 1.0, 0.0).astype(BF16)


def swap_blocks(exchange, read, write, count):
    for first in range(0, count, 2):
        pair = jnp.concatenate(
            [read(first).reshape(256, PIX), read(first + 1).reshape(256, PIX)], axis=1
        )
        moved = jnp.dot(exchange, pair, preferred_element_type=F32).astype(BF16)
        write(first, moved[:, :PIX].reshape(16, 16, PIX))
        write(first + 1, moved[:, PIX:].reshape(16, 16, PIX))


def block_number(patch, slot):
    return (slot & 1) * 128 + 2 * patch + (slot >> 1)


def pack_kernel(patch_ref, slot_ref, weight_ref, tile_ref, out_ref):
    exchange = exchange_matrix()
    count = tile_ref.shape[0]
    for half in range(2):
        for start in range(0, count, 16):

            def read(block):
                spot = half * HALF + block * 16
                return tile_ref[start : start + 16, spot : spot + 16, :]

            def write(block, value):
                spot = half * count + start
                out_ref[block * 16 : block * 16 + 16, spot : spot + 16, :] = value

            swap_blocks(exchange, read, write, HALF // 16)
    number = block_number(patch_ref[...], slot_ref[...]).astype(F32)
    weight = weight_ref[...].astype(F32)
    number = jnp.concatenate([number, number], axis=1)
    weight = jnp.concatenate([weight, weight], axis=1)
    row = lax.broadcasted_iota(jnp.int32, (META, PIX), 0)
    about = jnp.where(row == 0, number, jnp.where(row == 1, weight, 0.0)).astype(BF16)
    for device in range(out_ref.shape[0]):
        out_ref[device, 2 * count :, :] = about


def pack(patch, slot, weight, tiles):
    count = tiles.shape[0]
    return pl.pallas_call(
        pack_kernel,
        out_shape=jax.ShapeDtypeStruct((HALF, 2 * count + META, PIX), BF16),
        compiler_params=pltpu.CompilerParams(vmem_limit_bytes=24 * 1024 * 1024),
        cost_estimate=pl.CostEstimate(
            flops=4 * 256 * count * HALF * PIX, bytes_accessed=8 * count * HALF * PIX, transcendentals=0
        ),
    )(patch, slot, weight, tiles)


def smooth_kernel(tile_ref, smoother_ref, out_ref):
    smoother = smoother_ref[...]
    across = jnp.dot(
        tile_ref[...].reshape(-1, PIX), smoother, preferred_element_type=F32
    ).astype(BF16)
    for tile in range(tile_ref.shape[0]):
        out_ref[tile] = lax.dot_general(
            smoother,
            across[tile * PIX : (tile + 1) * PIX],
            (((0,), (0,)), ((), ())),
            preferred_element_type=F32,
        )


def smooth_tiles(tiles, smoother):
    count = tiles.shape[0]
    return pl.pallas_call(
        smooth_kernel,
        grid=(count // 8,),
        in_specs=[
            pl.BlockSpec((8, PIX, PIX), lambda g: (g, 0, 0)),
            pl.BlockSpec((PIX, PIX), lambda g: (0, 0)),
        ],
        out_specs=pl.BlockSpec((8, PIX, PIX), lambda g: (g, 0, 0)),
        out_shape=jax.ShapeDtypeStruct(tiles.shape, F32),
        cost_estimate=pl.CostEstimate(
            flops=4 * count * PIX**3, bytes_accessed=6 * count * PIX * PIX, transcendentals=0
        ),
    )(tiles, smoother)


def coadd_kernel(row_ref, coadd_ref, sum_ref):
    sources = row_ref.shape[0]
    count = (row_ref.shape[1] - META) // 2
    numbers = lax.broadcasted_iota(jnp.int32, (BINS, PIX), 0).astype(F32)
    first_source = lax.broadcasted_iota(jnp.int32, (META, PIX), 1) < count
    ones = jnp.ones((4 * count, PIX), BF16)
    running = jnp.zeros((BINS, 3 * PIX), F32)
    for first in range(0, sources, 4):
        loading = []
        for source in (first, first + 2):
            about = jnp.where(
                first_source,
                row_ref[source, 2 * count :, :].astype(F32),
                row_ref[source + 1, 2 * count :, :].astype(F32),
            )
            loading.append(jnp.where(about[0:1] == numbers, about[1:2], 0.0).astype(BF16))
        values = jnp.concatenate(
            [
                row_ref[first : first + 4, 0:count, :].reshape(4 * count, PIX),
                row_ref[first : first + 4, count : 2 * count, :].reshape(4 * count, PIX),
                ones,
            ],
            axis=1,
        )
        running = running + jnp.dot(
            jnp.concatenate(loading, axis=1), values, preferred_element_type=F32
        )
    weight_sum = running[:, 2 * PIX :]
    scale = jnp.maximum(weight_sum, 1.0)
    coadd_ref[0:BINS, :] = (running[:, :PIX] / scale).astype(BF16)
    coadd_ref[BINS:, :] = (running[:, PIX : 2 * PIX] / scale).astype(BF16)
    sum_ref[...] = weight_sum


def coadd_rows(rows):
    return pl.pallas_call(
        coadd_kernel,
        out_shape=(
            jax.ShapeDtypeStruct((2 * BINS, PIX), BF16),
            jax.ShapeDtypeStruct((BINS, PIX), F32),
        ),
        compiler_params=pltpu.CompilerParams(vmem_limit_bytes=24 * 1024 * 1024),
        cost_estimate=pl.CostEstimate(
            flops=6 * BINS * 4096 * PIX, bytes_accessed=4 * 4096 * PIX, transcendentals=0
        ),
    )(rows)


def detect_kernel(
    place_ref,
    coeff_ref,
    gathered_ref,
    tile_source,
    across_source,
    down_source,
    out_ref,
    image_ref,
    held_ref,
    tile_ref,
    across_ref,
    down_ref,
    arrived,
    *scratch,
):
    window_refs, mixed_refs = scratch[:BUFFERS], scratch[BUFFERS:]

    def piece(part):
        spot = pl.ds(part * 16, 16)
        return pltpu.make_async_copy(gathered_ref.at[spot], held_ref.at[spot], arrived.at[part])

    others = [
        pltpu.make_async_copy(source, target, arrived.at[HALF // 16 + number])
        for number, (source, target) in enumerate(
            ((tile_source, tile_ref), (across_source, across_ref), (down_source, down_ref))
        )
    ]
    for part in range(HALF // 16):
        piece(part).start()
    for other in others:
        other.start()
    exchange = exchange_matrix()
    lane = lax.broadcasted_iota(jnp.int32, (SPAN, PIX), 1)
    row = lax.broadcasted_iota(jnp.int32, (SPAN, PIX), 0)
    tile_count = out_ref.shape[0]

    def regroup(part, block, carry):
        base = pl.multiple_of(block * 16, 16)

        def read(half):
            start = pl.multiple_of(base + half * BINS, 16)
            return held_ref[part * 16 : part * 16 + 16, pl.ds(start, 16), :]

        def write(half, value):
            spot = half * HALF + part * 16
            image_ref[pl.ds(base, 16), spot : spot + 16, :] = value

        swap_blocks(exchange, read, write, 2)
        return carry

    for part in range(HALF // 16):
        piece(part).wait()
        lax.fori_loop(0, BINS // 16, functools.partial(regroup, part), 0, unroll=16)

    for other in others:
        other.wait()

    def group(number, window_ref, mixed_ref):
        for local in range(GROUP):
            place = place_ref[number * GROUP + local]
            column = place // 128
            level = place % 128
            other = place + 128 - 256 * column
            outside = ((level == 0) & (row < HALO)) | ((level == 127) & (row >= HALO + PIX))
            wrong_side = (lane // 64) != column
            back = jnp.where(level == 0, 0, 1)
            ahead = jnp.where(level == 127, 0, 1)
            for spot, block, unwanted in ((0, place, outside), (PIX, other, outside | wrong_side)):
                value = jnp.concatenate(
                    [
                        image_ref[block - back, PIX - HALO :, :],
                        image_ref[block],
                        image_ref[block + ahead, 0:HALO, :],
                    ],
                    axis=0,
                )
                value = jnp.where(unwanted, 0.0, value.astype(F32)).astype(BF16)
                window_ref[local * SPAN : (local + 1) * SPAN, spot : spot + PIX] = value
        window = window_ref[...]
        for scale in range(3):
            members = [k for k, pair in enumerate(PAIRS) if pair[0] == scale]
            first, last = members[0], members[-1] + 1
            filtered = jnp.dot(
                window, across_ref[:, first * PIX : last * PIX], preferred_element_type=F32
            )
            for local in range(GROUP):
                rows = slice(local * SPAN, (local + 1) * SPAN)
                base = (number * GROUP + local) * NB
                for power_y in range(DEGREES[scale] + 1):
                    total = None
                    for power_x in range(DEGREES[scale] + 1 - power_y):
                        scalar = coeff_ref[base + BASIS.index((scale, power_x, power_y))]
                        term = scalar * filtered[rows, power_x * PIX : (power_x + 1) * PIX]
                        total = term if total is None else total + term
                    spot = (first + power_y) * SPAN
                    mixed_ref[spot : spot + SPAN, local * PIX : (local + 1) * PIX] = total.astype(BF16)
        begin = pl.multiple_of(number * GROUP, GROUP)
        result = jnp.dot(down_ref[...], mixed_ref[...], preferred_element_type=F32)
        for local in range(GROUP):
            piece = result[:, local * PIX : (local + 1) * PIX] + tile_ref[begin + local]
            out_ref[begin + local] = piece.astype(BF16)

    def groups(number, carry):
        for which in range(BUFFERS):
            group(number * BUFFERS + which, window_refs[which], mixed_refs[which])
        return carry

    lax.fori_loop(0, tile_count // (GROUP * BUFFERS), groups, 0)


def detect(place, coeff, gathered, tiles, across, down):
    tile_count = tiles.shape[0]
    depth = down.shape[1]
    smem = pl.BlockSpec(memory_space=pltpu.SMEM)
    vmem = pl.BlockSpec(memory_space=pltpu.VMEM)
    return pl.pallas_call(
        detect_kernel,
        in_specs=[smem, smem] + [pl.BlockSpec(memory_space=pl.ANY)] * 4,
        out_specs=vmem,
        out_shape=jax.ShapeDtypeStruct((tile_count, PIX, PIX), BF16),
        scratch_shapes=[
            pltpu.VMEM((BINS, PIX, PIX), BF16),
            pltpu.VMEM(gathered.shape, BF16),
            pltpu.VMEM(tiles.shape, F32),
            pltpu.VMEM(across.shape, BF16),
            pltpu.VMEM(down.shape, BF16),
            pltpu.SemaphoreType.DMA((HALF // 16 + 3,)),
        ]
        + [pltpu.VMEM((GROUP * SPAN, 2 * PIX), BF16)] * BUFFERS
        + [pltpu.VMEM((depth, GROUP * PIX), BF16)] * BUFFERS,
        compiler_params=pltpu.CompilerParams(vmem_limit_bytes=60 * 1024 * 1024),
        cost_estimate=pl.CostEstimate(
            flops=2 * tile_count * (SPAN * 256 * 1408 + depth * PIX * PIX),
            bytes_accessed=12 * 1024 * 1024,
            transcendentals=0,
        ),
    )(place, coeff, gathered, tiles, across, down)


def body(visit_tiles, tile_patch, tile_slot, tile_weight, psf_coeff):
    tiles = visit_tiles[0]
    across, down, smoother = (jnp.asarray(m) for m in constants())
    patch = lax.axis_index("patch")
    patch_count = lax.axis_size("patch")
    band_count = lax.axis_size("band")
    tile_patch = tile_patch.reshape(tile_slot.shape)
    place = block_number(tile_patch[0], tile_slot[0])
    coeff = psf_coeff[0].astype(F32).reshape(-1)

    def exchanged(array, axis):
        return lax.all_to_all(array, axis, split_axis=0, concat_axis=0, tiled=True)

    rows = exchanged(pack(tile_patch, tile_slot, tile_weight, tiles), "patch")
    coadd, weight_sum = coadd_rows(rows)
    gathered = lax.all_gather(coadd, "patch", axis=0, tiled=False)

    own = coadd.reshape(4, patch_count, 2, PIX).transpose(1, 0, 2, 3).reshape(patch_count, 8, PIX)
    own = exchanged(own, "patch").reshape(HALF, 2, 2, 2, PIX)
    coadd_image = own.transpose(3, 1, 0, 2, 4)
    own_sum = lax.dynamic_slice_in_dim(weight_sum.reshape(2, 128, PIX), 2 * patch, 2, axis=1)
    own_sum = own_sum.transpose(1, 0, 2)[:, None, None]
    coadd_float = coadd_image.astype(F32)
    terms = (own_sum * coadd_float * coadd_float).reshape(SB * PIX, SB * PIX).astype(BF16)
    terms = exchanged(jnp.broadcast_to(terms[None], (band_count,) + terms.shape), "band")
    chi_image = jnp.sqrt(1.0 + jnp.sum(terms.astype(F32), axis=0)).astype(BF16)
    coadd_image = coadd_image.reshape(1, SB * PIX, SB * PIX)

    later, coadd = lax.optimization_barrier((tiles, coadd))
    smoothed = smooth_tiles(later, smoother)
    gathered, smoothed, chi_image, coadd_image = lax.optimization_barrier(
        (gathered, smoothed, chi_image, coadd_image)
    )
    detection = detect(place, coeff, gathered, smoothed, across, down)
    return (coadd_image, detection[None], chi_image)


def solution(mesh):
    return jax.shard_map(
        body,
        mesh=mesh,
        in_specs=(
            P("band", "patch", None, None),
            P("band", "patch", None),
            P("band", "patch"),
            P("band", "patch"),
            P("band", "patch", None),
        ),
        out_specs=(P("band", "patch", None), P("band", "patch", None, None), P("patch", None)),
        check_vma=False,
    )
```

```python
import functools

import jax
import jax.numpy as jnp
import ml_dtypes
import numpy as np
from jax import lax
from jax.experimental import pallas as pl
from jax.experimental.pallas import tpu as pltpu
from jax.sharding import PartitionSpec as P

KR = 10
SB = 2
PIX = 128
HALF = 64
HALO = 16
SPAN = PIX + 2 * HALO
META = 16
BINS = 256
GROUP = 4
BUFFERS = 2
NB = 27
SIGMAS = (0.7, 1.5, 3.0)
DEGREES = (4, 2, 2)
BF16 = jnp.bfloat16
F32 = jnp.float32

PAIRS = [(s, p) for s in range(3) for p in range(DEGREES[s] + 1)]
BASIS = [
    (s, i, j)
    for s in range(3)
    for i in range(DEGREES[s] + 1)
    for j in range(DEGREES[s] + 1 - i)
]


def rounded(values):
    return np.asarray(values, np.float32).astype(ml_dtypes.bfloat16)


def kernel_taps(sigma_value, exponent):
    offsets = np.arange(-KR, KR + 1).astype(np.float32)
    gaussian = np.exp(-offsets * offsets / np.float32(2.0 * sigma_value * sigma_value))
    taps = gaussian * (offsets / np.float32(sigma_value)) ** exponent / np.sum(gaussian)
    return rounded(taps).astype(np.float64)


def smooth_taps():
    offsets = np.arange(-KR, KR + 1).astype(np.float32)
    gaussian = np.exp(-offsets * offsets / np.float32(8.0))
    return rounded(gaussian / np.sum(gaussian)).astype(np.float64)


def tap_matrix(taps, source, target):
    distance = source[:, None] - target[None, :]
    inside = np.abs(distance) <= KR
    return np.where(inside, taps[np.clip(distance + KR, 0, 2 * KR)], 0.0)


def constants():
    pixel = np.arange(PIX)
    smoother = tap_matrix(smooth_taps(), pixel, pixel)
    columns = np.concatenate([pixel, PIX + np.arange(64), np.arange(64) - 64])
    across = np.concatenate(
        [tap_matrix(kernel_taps(SIGMAS[s], i), columns, pixel) @ smoother.T for s, i in PAIRS], axis=1
    )
    rows = np.arange(SPAN) - HALO
    down = [-(smoother @ tap_matrix(kernel_taps(SIGMAS[s], j), rows, pixel).T) for s, j in PAIRS]
    return rounded(across), rounded(np.concatenate(down + [smoother], axis=1)), rounded(smoother.T)


def exchange_matrix():
    order = np.arange(256).reshape(16, 16).T.reshape(256)
    return np.eye(256, dtype=np.float32)[order].astype(ml_dtypes.bfloat16)


def swap_blocks(exchange, read, write, count):
    for first in range(0, count, 2):
        pair = jnp.concatenate(
            [read(first).reshape(256, PIX), read(first + 1).reshape(256, PIX)], axis=1
        )
        moved = jnp.dot(exchange, pair, preferred_element_type=F32).astype(BF16)
        write(first, moved[:, :PIX].reshape(16, 16, PIX))
        write(first + 1, moved[:, PIX:].reshape(16, 16, PIX))


def pack_kernel(about_ref, tile_ref, out_ref):
    target = lax.broadcasted_iota(jnp.int32, (256, 256), 0)
    origin = lax.broadcasted_iota(jnp.int32, (256, 256), 1)
    exchange = jnp.where(origin == (target % 16) * 16 + target // 16, 1.0, 0.0).astype(BF16)
    count = tile_ref.shape[0]
    for half in range(2):
        for start in range(0, count, 16):

            def read(block):
                spot = half * HALF + block * 16
                return tile_ref[start : start + 16, spot : spot + 16, :]

            def write(block, value):
                spot = half * count + start
                out_ref[block * 16 : block * 16 + 16, spot : spot + 16, :] = value

            swap_blocks(exchange, read, write, HALF // 16)
    about = about_ref[...]
    for device in range(out_ref.shape[0]):
        out_ref[device, 2 * count :, :] = about


def pack(about, tiles):
    count = tiles.shape[0]
    return pl.pallas_call(
        pack_kernel,
        out_shape=jax.ShapeDtypeStruct((HALF, 2 * count + META, PIX), BF16),
        compiler_params=pltpu.CompilerParams(vmem_limit_bytes=24 * 1024 * 1024),
        cost_estimate=pl.CostEstimate(
            flops=4 * 256 * count * HALF * PIX, bytes_accessed=8 * count * HALF * PIX, transcendentals=0
        ),
    )(about, tiles)


def coadd_kernel(row_ref, coadd_ref, sum_ref):
    sources = row_ref.shape[0]
    count = (row_ref.shape[1] - META) // 2
    numbers = lax.broadcasted_iota(jnp.int32, (BINS, PIX), 0).astype(F32)
    ones = jnp.ones((4 * count, PIX), BF16)
    running = jnp.zeros((BINS, 3 * PIX), F32)
    for first in range(0, sources, 4):
        loading = []
        for source in (first, first + 2):
            about = row_ref[source, 2 * count :, :].astype(F32) + row_ref[source + 1, 2 * count :, :].astype(F32)
            loading.append(jnp.where(about[0:1] == numbers, about[1:2], 0.0).astype(BF16))
        values = jnp.concatenate(
            [
                row_ref[first : first + 4, 0:count, :].reshape(4 * count, PIX),
                row_ref[first : first + 4, count : 2 * count, :].reshape(4 * count, PIX),
                ones,
            ],
            axis=1,
        )
        running = running + jnp.dot(
            jnp.concatenate(loading, axis=1), values, preferred_element_type=F32
        )
    weight_sum = running[:, 2 * PIX :]
    scale = jnp.maximum(weight_sum, 1.0)
    coadd_ref[0:BINS, :] = (running[:, :PIX] / scale).astype(BF16)
    coadd_ref[BINS:, :] = (running[:, PIX : 2 * PIX] / scale).astype(BF16)
    sum_ref[...] = weight_sum


def coadd_rows(rows):
    return pl.pallas_call(
        coadd_kernel,
        out_shape=(
            jax.ShapeDtypeStruct((2 * BINS, PIX), BF16),
            jax.ShapeDtypeStruct((BINS, PIX), F32),
        ),
        compiler_params=pltpu.CompilerParams(vmem_limit_bytes=24 * 1024 * 1024),
        cost_estimate=pl.CostEstimate(
            flops=6 * BINS * 4096 * PIX, bytes_accessed=4 * 4096 * PIX, transcendentals=0
        ),
    )(rows)


def detect_kernel(
    place_ref,
    coeff_ref,
    exchange_ref,
    gathered_ref,
    tile_source,
    across_source,
    down_source,
    smoother_ref,
    out_ref,
    image_ref,
    held_ref,
    tile_ref,
    across_ref,
    down_ref,
    arrived,
    *scratch,
):
    window_refs, mixed_refs = scratch[:BUFFERS], scratch[BUFFERS:]

    def piece(part):
        spot = pl.ds(part * 16, 16)
        return pltpu.make_async_copy(gathered_ref.at[spot], held_ref.at[spot], arrived.at[part])

    others = [
        pltpu.make_async_copy(source, target, arrived.at[HALF // 16 + number])
        for number, (source, target) in enumerate(
            ((tile_source, tile_ref), (across_source, across_ref), (down_source, down_ref))
        )
    ]
    for part in range(HALF // 16):
        piece(part).start()
    for other in others:
        other.start()
    exchange = exchange_ref[...]
    lane = lax.broadcasted_iota(jnp.int32, (SPAN, PIX), 1)
    row = lax.broadcasted_iota(jnp.int32, (SPAN, PIX), 0)
    tile_count = out_ref.shape[0]

    def regroup(part, block, carry):
        base = pl.multiple_of(block * 16, 16)

        def read(half):
            start = pl.multiple_of(base + half * BINS, 16)
            return held_ref[part * 16 : part * 16 + 16, pl.ds(start, 16), :]

        def write(half, value):
            spot = half * HALF + part * 16
            image_ref[pl.ds(base, 16), spot : spot + 16, :] = value

        swap_blocks(exchange, read, write, 2)
        return carry

    for part in range(HALF // 16):
        piece(part).wait()
        lax.fori_loop(0, BINS // 16, functools.partial(regroup, part), 0, unroll=16)

    for other in others:
        other.wait()

    def group(number, window_ref, mixed_ref):
        for local in range(GROUP):
            place = place_ref[number * GROUP + local]
            column = place // 128
            level = place % 128
            other = place + 128 - 256 * column
            outside = ((level == 0) & (row < HALO)) | ((level == 127) & (row >= HALO + PIX))
            wrong_side = (lane // 64) != column
            back = jnp.where(level == 0, 0, 1)
            ahead = jnp.where(level == 127, 0, 1)
            for spot, block, unwanted in ((0, place, outside), (PIX, other, outside | wrong_side)):
                value = jnp.concatenate(
                    [
                        image_ref[block - back, PIX - HALO :, :],
                        image_ref[block],
                        image_ref[block + ahead, 0:HALO, :],
                    ],
                    axis=0,
                )
                value = jnp.where(unwanted, 0.0, value.astype(F32)).astype(BF16)
                window_ref[local * SPAN : (local + 1) * SPAN, spot : spot + PIX] = value
        window = window_ref[...]
        for scale in range(3):
            members = [k for k, pair in enumerate(PAIRS) if pair[0] == scale]
            first, last = members[0], members[-1] + 1
            filtered = jnp.dot(
                window, across_ref[:, first * PIX : last * PIX], preferred_element_type=F32
            )
            for local in range(GROUP):
                rows = slice(local * SPAN, (local + 1) * SPAN)
                base = (number * GROUP + local) * NB
                for power_y in range(DEGREES[scale] + 1):
                    total = None
                    for power_x in range(DEGREES[scale] + 1 - power_y):
                        scalar = coeff_ref[base + BASIS.index((scale, power_x, power_y))]
                        term = scalar * filtered[rows, power_x * PIX : (power_x + 1) * PIX]
                        total = term if total is None else total + term
                    spot = (first + power_y) * SPAN
                    mixed_ref[spot : spot + SPAN, local * PIX : (local + 1) * PIX] = total.astype(BF16)
        begin = pl.multiple_of(number * GROUP, GROUP)
        tiles = tile_ref[pl.ds(begin, GROUP)].reshape(GROUP * PIX, PIX)
        smooth = jnp.dot(tiles, smoother_ref[...], preferred_element_type=F32).astype(BF16)
        spot = len(PAIRS) * SPAN
        for local in range(GROUP):
            mixed_ref[spot : spot + PIX, local * PIX : (local + 1) * PIX] = smooth[
                local * PIX : (local + 1) * PIX
            ]
        result = jnp.dot(down_ref[...], mixed_ref[...], preferred_element_type=F32)
        for local in range(GROUP):
            out_ref[begin + local] = result[:, local * PIX : (local + 1) * PIX].astype(BF16)

    def groups(number, carry):
        for which in range(BUFFERS):
            group(number * BUFFERS + which, window_refs[which], mixed_refs[which])
        return carry

    lax.fori_loop(0, tile_count // (GROUP * BUFFERS), groups, 0)


def detect(place, coeff, exchange, gathered, tiles, across, down, smoother):
    tile_count = tiles.shape[0]
    depth = down.shape[1]
    smem = pl.BlockSpec(memory_space=pltpu.SMEM)
    vmem = pl.BlockSpec(memory_space=pltpu.VMEM)
    return pl.pallas_call(
        detect_kernel,
        in_specs=[smem, smem, vmem] + [pl.BlockSpec(memory_space=pl.ANY)] * 4 + [vmem],
        out_specs=vmem,
        out_shape=jax.ShapeDtypeStruct((tile_count, PIX, PIX), BF16),
        scratch_shapes=[
            pltpu.VMEM((BINS, PIX, PIX), BF16),
            pltpu.VMEM(gathered.shape, BF16),
            pltpu.VMEM(tiles.shape, BF16),
            pltpu.VMEM(across.shape, BF16),
            pltpu.VMEM(down.shape, BF16),
            pltpu.SemaphoreType.DMA((HALF // 16 + 3,)),
        ]
        + [pltpu.VMEM((GROUP * SPAN, 2 * PIX), BF16)] * BUFFERS
        + [pltpu.VMEM((depth, GROUP * PIX), BF16)] * BUFFERS,
        compiler_params=pltpu.CompilerParams(vmem_limit_bytes=48 * 1024 * 1024),
        cost_estimate=pl.CostEstimate(
            flops=2 * tile_count * (SPAN * 256 * 1408 + depth * PIX * PIX),
            bytes_accessed=12 * 1024 * 1024,
            transcendentals=0,
        ),
    )(place, coeff, exchange, gathered, tiles, across, down, smoother)


def body(visit_tiles, tile_patch, tile_slot, tile_weight, psf_coeff):
    tiles = visit_tiles[0]
    across, down, smoother = (jnp.asarray(m) for m in constants())
    exchange = jnp.asarray(exchange_matrix())
    patch = lax.axis_index("patch")
    patch_count = lax.axis_size("patch")
    band_count = lax.axis_size("band")
    place = (tile_slot[0] % 2) * 128 + 2 * tile_patch[0, :, 0] + tile_slot[0] // 2
    facts = jnp.stack([place.astype(F32), tile_weight[0].astype(F32)])
    even = (patch % 2) == 0
    facts = jnp.concatenate([jnp.where(even, facts, 0.0), jnp.where(even, 0.0, facts)], axis=1)
    about = jnp.pad(facts, ((0, META - 2), (0, 0))).astype(BF16)
    coeff = psf_coeff[0].astype(F32).reshape(-1)

    def exchanged(array, axis):
        return lax.all_to_all(array, axis, split_axis=0, concat_axis=0, tiled=True)

    rows = exchanged(pack(about, tiles), "patch")
    coadd, weight_sum = coadd_rows(rows)
    gathered = lax.all_gather(coadd, "patch", axis=0, tiled=False)

    own = coadd.reshape(4, patch_count, 2, PIX).transpose(1, 0, 2, 3).reshape(patch_count, 8, PIX)
    own = exchanged(own, "patch").reshape(HALF, 2, 2, 2, PIX)
    coadd_image = own.transpose(3, 1, 0, 2, 4)
    own_sum = lax.dynamic_slice_in_dim(weight_sum.reshape(2, 128, PIX), 2 * patch, 2, axis=1)
    own_sum = own_sum.transpose(1, 0, 2)[:, None, None]
    coadd_float = coadd_image.astype(F32)
    terms = (own_sum * coadd_float * coadd_float).reshape(SB * PIX, SB * PIX).astype(BF16)
    terms = exchanged(jnp.broadcast_to(terms[None], (band_count,) + terms.shape), "band")
    chi_image = jnp.sqrt(1.0 + jnp.sum(terms.astype(F32), axis=0)).astype(BF16)
    coadd_image = coadd_image.reshape(1, SB * PIX, SB * PIX)

    gathered, chi_image, coadd_image = lax.optimization_barrier((gathered, chi_image, coadd_image))
    detection = detect(place, coeff, exchange, gathered, tiles, across, down, smoother)
    return (coadd_image, detection[None], chi_image)


def solution(mesh):
    return jax.shard_map(
        body,
        mesh=mesh,
        in_specs=(
            P("band", "patch", None, None),
            P("band", "patch", None),
            P("band", "patch"),
            P("band", "patch"),
            P("band", "patch", None),
        ),
        out_specs=(P("band", "patch", None), P("band", "patch", None, None), P("patch", None)),
        check_vma=False,
    )
```
